256 devices in a mesh: rows: 16 (over y_lo, z), blk: 16 (over x, y_hi, core).
Axes of the slice: x: 4, y: 4 (y_hi: 2, y_lo: 2; y = y_hi * 2 + y_lo), z: 8, core: 2. Of those that a mesh axis runs over, the one named last changes fastest.
Arguments:
- hidden: bfloat16 [262144, 256], P(('rows', 'blk')), may hold values from -6 to 6
- weight: bfloat16 [256, 256], replicated, may hold values from -0.375 to 0.375
- adjacency: bfloat16 [8192, 128, 128], P(('rows', 'blk')), may hold values from -0.3125 to 0.3125
- tile_target: int32 [8192], P(('rows', 'blk')), may hold values from 0 to 128, as said below
- tile_source: int32 [8192], P(('rows', 'blk')), may hold values from 0 to 128, as said below
- upstream: bfloat16 [262144, 256], P(('rows', 'blk')), may hold values from -6 to 6
- labels: int32 [262144], P(('rows', 'blk')), may hold values 0 or 1
Outputs:
- output: bfloat16 [262144, 256], P(('rows', 'blk'))
- d_hidden: bfloat16 [262144, 256], P(('rows', 'blk'))
- d_weight: float32 [256, 256], replicated
The draws below stay inside these ranges and needn't reach their ends.
Inputs may be any that keep to these rules, and one draw needn't show every extreme that they name: The value 16 * 8 marks an empty slot, and exactly the same slots are empty in tile_source. Every device uses between 16 and 32 slots, some device uses all 32 and some device exactly 16. Of one device's used slots at most 2 have the same tile_target // 8, and some device reaches 2. The same pair of indices may occur in several slots. `tile_source`: the value 16 * 8 marks an empty slot, exactly where tile_target is 128.
All inputs are finite; a program needn't handle non-finite values. No bound on the sum of `labels` on one device may be relied on, other than what follows from the above.
Results may differ from the reference program's by a relative error of at most 0.02.
Values may be sent and summed in bfloat16 or wider, within the bound.
No kernel may reach another device: no remote copies, remote signals or barrier semaphores. Data moves between devices by JAX's collectives and lax.ppermute only.
A program may use at most 128 MiB of HBM per device.

```python
import math
import jax
import jax.numpy as jnp
from jax import lax

HID = 256
BLOCK = 128
NBD = 8
TPB = 4
TILES = 32
NODES = 262144
N_ROWS = 16
N_BLK = 16


def tile_lists(key):
    device_count = N_ROWS * N_BLK
    key_list = jax.random.split(key, 8)
    counts = jax.random.randint(key_list[0], (device_count,), TILES // 2, TILES + 1)
    fullest = jax.random.randint(key_list[1], (), 0, device_count)
    lightest = (fullest + 1 + jax.random.randint(key_list[2], (), 0, device_count - 1)) % device_count
    device_ids = jnp.arange(device_count)
    counts = jnp.where(device_ids == fullest, TILES, jnp.where(device_ids == lightest, TILES // 2, counts))
    peer_order = jax.vmap(lambda k: jax.random.permutation(k, N_ROWS))(jax.random.split(key_list[3], device_count))
    slot_order = jax.vmap(lambda k: jax.random.permutation(k, TILES))(jax.random.split(key_list[4], device_count))
    pair_ids = slot_order // 2 % N_ROWS
    peers = jnp.take_along_axis(peer_order, pair_ids, axis=1)
    live_rank = jax.vmap(lambda k: jax.random.permutation(k, TILES))(jax.random.split(key_list[5], device_count))
    live_mask = live_rank < counts[:, None]
    local = jax.random.randint(key_list[6], (device_count, TILES), 0, NBD)
    source = jax.random.randint(key_list[7], (device_count, TILES), 0, N_BLK * NBD)
    target = jnp.where(live_mask, peers * NBD + local, N_ROWS * NBD)
    source = jnp.where(live_mask, source, N_BLK * NBD)
    return (target.reshape(-1).astype(jnp.int32), source.reshape(-1).astype(jnp.int32))


def draw_tile_target(key, part):
    lists = tile_lists(key)
    return lists[0]


def draw_tile_source(key, part):
    lists = tile_lists(key)
    return lists[1]


def with_ends(entries, key, least, high):
    index_at = [jax.random.randint(jax.random.fold_in(key, axis), (), 0, length) for axis, length in enumerate(entries.shape)]
    widest = entries.shape.index(max(entries.shape))
    beside = index_at[:widest] + [(index_at[widest] + 1) % entries.shape[widest]] + index_at[widest + 1:]
    return entries.at[tuple(index_at)].set(least).at[tuple(beside)].set(high)


def shard_levels(key, shape, shards, least, top_value):
    loudness = 1.0
    for position, blocks in shards:
        heights = jax.random.uniform(jax.random.fold_in(jax.random.fold_in(key, 6), position), (blocks,), jnp.float32, least / len(shards), top_value / len(shards))
        loudness = loudness * jnp.repeat(jnp.exp(heights), shape[position] // blocks).reshape((-1,) + (1,) * (len(shape) - 1 - position))
    return loudness


def noise(own_key, extent, deviation, limit, cuts=(), held_as=jnp.bfloat16):
    result = deviation * jax.random.normal(own_key, extent, jnp.float32)
    if cuts:
        result = result * shard_levels(own_key, extent, cuts, -0.22, 0.18)
    return jnp.clip(result, -limit, limit).astype(held_as)


def setup_inputs(seed: int = 0) -> dict:
    key_of = jax.random.split(jax.random.key(seed), 8)
    return {
        "hidden": noise(key_of[0], (NODES, HID), 1.0, 6.0, ((0, 256),)),
        "weight": noise(key_of[1], (HID, HID), HID ** -0.5, 0.375),
        "adjacency": noise(key_of[2], (N_ROWS * N_BLK * TILES, BLOCK, BLOCK), (BLOCK * TPB * 3 // 4) ** -0.5, 0.3125, ((0, 256),)),
        "tile_target": draw_tile_target(jax.random.fold_in(key_of[7], 71), 0),
        "tile_source": draw_tile_source(jax.random.fold_in(key_of[7], 71), 0),
        "upstream": noise(key_of[5], (NODES, HID), 1.0, 6.0, ((0, 256),)),
        "labels": with_ends((jax.random.randint(key_of[6], (NODES,), 0, 2) < 1).astype(jnp.int32), jax.random.fold_in(key_of[6], 1), 0, 1),
    }


def silu_slope(values):
    logistic = jax.nn.sigmoid(values)
    return logistic * (1.0 + values * (1.0 - logistic))

def round_keep(values):
    rounded = lax.optimization_barrier(values.astype(jnp.bfloat16))
    return rounded.astype(jnp.float32)

def reference(hidden, weight, adjacency, tile_target, tile_source, upstream, labels):
    block_count = NODES // BLOCK
    column_count = N_ROWS * NBD
    panel_count = N_BLK * NBD
    device_count = N_ROWS * N_BLK
    local_ids = jnp.arange(NBD, dtype=jnp.int32)

    def column_ids(blk_index):
        rows_part = jnp.arange(N_ROWS, dtype=jnp.int32)[:, None] * N_BLK + blk_index
        return (rows_part * NBD + local_ids[None, :]).reshape(-1).astype(jnp.int32)

    def panel_ids(row_index):
        blk_part = row_index * N_BLK + jnp.arange(N_BLK, dtype=jnp.int32)[:, None]
        return (blk_part * NBD + local_ids[None, :]).reshape(-1).astype(jnp.int32)
    projected = jnp.dot(hidden, weight, preferred_element_type=jnp.float32).astype(jnp.bfloat16)
    projected = projected.reshape(block_count, BLOCK, HID)
    tiles_all = adjacency.reshape(device_count, TILES, BLOCK, BLOCK)
    targets = tile_target.reshape(device_count, TILES)
    sources = tile_source.reshape(device_count, TILES)
    devices = jnp.arange(device_count, dtype=jnp.int32)

    def forward(running, scan_item):
        device, tile_blocks, target, source = scan_item
        row_index = device // N_BLK
        blk_index = device % N_BLK
        source_ids = panel_ids(row_index)[jnp.minimum(source, panel_count - 1)]
        gathered = projected[source_ids].astype(jnp.float32)
        product = jnp.einsum('tij,tjf->tif', tile_blocks.astype(jnp.float32), gathered)
        partial_sum = jax.ops.segment_sum(product, target, column_count + 1)[:column_count]
        running = running.at[column_ids(blk_index)].add(round_keep(partial_sum))
        return (running, None)
    summed = lax.scan(forward, jnp.zeros((block_count, BLOCK, HID), jnp.float32), (devices, tiles_all, targets, sources))[0]
    summed = summed.reshape(NODES, HID)
    output = jax.nn.silu(summed).astype(jnp.bfloat16)
    grad_rows = upstream.astype(jnp.float32) * labels.astype(jnp.float32)[:, None] * silu_slope(summed)
    grad_blocks = grad_rows.astype(jnp.bfloat16).reshape(block_count, BLOCK, HID)

    def backward(running, scan_item):
        device, tile_blocks, target, source = scan_item
        row_index = device // N_BLK
        blk_index = device % N_BLK
        target_ids = column_ids(blk_index)[jnp.minimum(target, column_count - 1)]
        picked = grad_blocks[target_ids].astype(jnp.float32)
        back_prod = jnp.einsum('tji,tjf->tif', tile_blocks.astype(jnp.float32), picked)
        back_sum = jax.ops.segment_sum(back_prod, source, panel_count + 1)[:panel_count]
        running = running.at[panel_ids(row_index)].add(round_keep(back_sum))
        return (running, None)
    d_sum = lax.scan(backward, jnp.zeros((block_count, BLOCK, HID), jnp.float32), (devices, tiles_all, targets, sources))[0]
    d_proj = d_sum.reshape(NODES, HID).astype(jnp.bfloat16)
    d_hidden = lax.dot_general(d_proj, weight, (((1,), (1,)), ((), ())), preferred_element_type=jnp.float32).astype(jnp.bfloat16)
    d_weight = jnp.dot(hidden.T, d_proj, preferred_element_type=jnp.float32) * (1.0 / math.sqrt(NODES))
    return (output, d_hidden, d_weight)
```

```python
import math

import jax
import jax.numpy as jnp
from jax import lax
from jax.experimental import pallas as pl
from jax.experimental.pallas import tpu as pltpu
from jax.sharding import PartitionSpec as P

BF16 = jnp.bfloat16
F32 = jnp.float32
CHUNKS = 1
VMEM_BYTES = 56 * 1024 * 1024


def blk_pairs(blk_count, dx, dy, dc):
    x_count = blk_count // 4
    pairs = []
    for b in range(blk_count):
        x, y, c = b // 4, (b // 2) % 2, b % 2
        pairs.append((b, ((x + dx) % x_count) * 4 + ((y + dy) % 2) * 2 + (c + dc) % 2))
    return pairs


def vmem(count):
    return [pl.BlockSpec(memory_space=pltpu.VMEM)] * count


def smem(count):
    return [pl.BlockSpec(memory_space=pltpu.SMEM)] * count


def forward_kernel(slot_ref, source_ref, tiles_ref, *refs):
    shards, out_ref = refs[:-4], refs[-4]
    held, tiles, sems = refs[-3:]
    copies = [pltpu.make_async_copy(tiles_ref, tiles, sems.at[len(shards)])]
    for k, shard in enumerate(shards):
        copies.append(pltpu.make_async_copy(shard, held.at[k], sems.at[k]))
    for copy in copies:
        copy.start()
    for copy in copies:
        copy.wait()
    block = tiles.shape[1]

    def step(s, carry):
        slot = slot_ref[s]
        source = jnp.maximum(source_ref[s], 0)

        @pl.when(slot >= 0)
        def _():
            panel = held[source // 8, pl.ds(pl.multiple_of((source % 8) * block, block), block), :]
            out_ref[s] = jnp.dot(tiles[slot], panel, preferred_element_type=F32).astype(BF16)

        @pl.when(slot < 0)
        def _():
            out_ref[s] = jnp.zeros(out_ref.shape[1:], BF16)

        return carry

    lax.fori_loop(0, out_ref.shape[0], step, 0)


def owner_kernel(local_ref, *refs):
    terms, (weight_ref, up_ref, out_ref) = refs[:CHUNKS], refs[CHUNKS : CHUNKS + 3]
    send_refs, (dw_ref, total) = refs[CHUNKS + 3 : -2], refs[-2:]
    block = terms[0].shape[1]
    width = terms[0].shape[2]
    total[...] = jnp.zeros(total.shape, F32)

    def add(s, carry):
        local = local_ref[s]

        @pl.when(local >= 0)
        def _():
            rows = pl.ds(pl.multiple_of(local * block, block), block)
            for k, term in enumerate(terms):
                cols = slice(k * width, (k + 1) * width)
                total[rows, cols] = total[rows, cols] + term[s].astype(F32)

        return carry

    lax.fori_loop(0, terms[0].shape[0], add, 0)
    weight = weight_ref[...]
    grads = []
    dw = jnp.zeros(dw_ref.shape, F32)
    for g in range(total.shape[0] // block):
        rows = slice(g * block, (g + 1) * block)
        aggregated = total[rows, :].astype(BF16)
        summed = jnp.dot(aggregated, weight, preferred_element_type=F32)
        logistic = jax.nn.sigmoid(summed)
        out_ref[rows, :] = (summed * logistic).astype(BF16)
        slope = logistic * (1.0 + summed * (1.0 - logistic))
        grad = (up_ref[rows, :].astype(F32) * slope).astype(BF16)
        total[rows, :] = grad.astype(F32)
        dw = dw + lax.dot_general(
            aggregated, grad, (((0,), (0,)), ((), ())), preferred_element_type=F32
        )
    dw_ref[...] = dw

    def lay(s, carry):
        local = jnp.maximum(local_ref[s], 0)
        rows = pl.ds(pl.multiple_of(local * block, block), block)
        for k, send in enumerate(send_refs):
            send[s] = total[rows, k * width : (k + 1) * width].astype(BF16)
        return carry

    lax.fori_loop(0, terms[0].shape[0], lay, 0)


def backward_kernel(slot_ref, place_ref, tiles_ref, far_tiles_ref, grads_ref, far_grads_ref, *refs):
    outs, total = refs[:-1], refs[-1]
    total[...] = jnp.zeros(total.shape, F32)
    half = tiles_ref.shape[0]

    def run(tiles, grads, base):
        def step(s, carry):
            place = place_ref[base + s]

            @pl.when(place >= 0)
            def _():
                slot = slot_ref[base + s]
                total[place] = total[place] + lax.dot_general(
                    tiles[slot], grads[s], (((0,), (0,)), ((), ())), preferred_element_type=F32
                )

            return carry

        lax.fori_loop(0, half, step, 0)

    run(tiles_ref, grads_ref, 0)
    run(far_tiles_ref, far_grads_ref, half)
    block = total.shape[1]
    per = outs[0].shape[0] // block
    for k, out in enumerate(outs):
        for g in range(per):
            out[g * block : (g + 1) * block, :] = total[k * per + g].astype(BF16)


def body(hidden, weight, adjacency, tile_target, tile_source, upstream, labels):
    block = adjacency.shape[1]
    slots = adjacency.shape[0]
    own_rows, width = hidden.shape
    own_blocks = own_rows // block
    row_count = lax.axis_size("rows")
    blk_count = lax.axis_size("blk")
    share = width // CHUNKS
    me = lax.axis_index("blk")
    move = lambda value, dx, dy, dc: lax.ppermute(value, "blk", blk_pairs(blk_count, dx, dy, dc))

    order = jnp.arange(slots, dtype=jnp.int32)
    peer = tile_target // own_blocks
    earlier = (peer[:, None] == peer[None, :]) & (order[None, :] < order[:, None])
    rank = jnp.sum(earlier.astype(jnp.int32), axis=1)
    spot = jnp.where(peer < row_count, peer * 2 + rank, -1)
    at = (spot[:, None] == order[None, :]).astype(jnp.int32)
    slot_at = jnp.sum(at * (order[:, None] + 1), axis=0) - 1
    local_at = jnp.sum(at * (tile_target[:, None] % own_blocks + 1), axis=0) - 1
    source_at = jnp.sum(at * (tile_source[:, None] + 1), axis=0) - 1
    holder = source_at // own_blocks
    dx = (holder // 4 - me // 4) % 4
    dy = (holder // 2 - me // 2) % 2
    dc = (holder - me) % 2
    inner = (dy * 4 + dx) * own_blocks + source_at % own_blocks
    panel_at = jnp.where(source_at >= 0, dc * (8 * own_blocks) + inner, -1)
    near_place = jnp.where((source_at >= 0) & (dc == 0), inner, -1)
    cross_place = jnp.where((source_at >= 0) & (dc == 1), inner, -1)

    local_send = jnp.broadcast_to(local_at.reshape(row_count, 2, 1), (row_count, 2, 128))
    local_got = lax.all_to_all(local_send, "rows", 0, 0, tiled=True)[:, :, 0].reshape(-1)
    far = move(jnp.stack([slot_at, cross_place]), 0, 0, 1)
    slot_both = jnp.concatenate([slot_at, far[0]])
    place_both = jnp.concatenate([near_place, far[1]])
    far_tiles = move(adjacency, 0, 0, 1)
    marked = upstream * labels.astype(BF16)[:, None]

    def gather(own):
        plus = move(own, -1, 0, 0)
        minus = move(own, 1, 0, 0)
        across = move(own, 0, 1, 0)
        twice = move(own, 2, 0, 0)
        across_minus = move(across, 1, 0, 0)
        across_plus = move(across, -1, 0, 0)
        across_twice = move(twice, 0, 1, 0)
        near = [own, plus, twice, minus, across, across_plus, across_twice, across_minus]
        return near + [move(value, 0, 0, 1) for value in near]

    def forward(shards):
        return pl.pallas_call(
            forward_kernel,
            out_shape=jax.ShapeDtypeStruct((slots, block, share), BF16),
            in_specs=smem(2) + [pl.BlockSpec(memory_space=pl.ANY)] * (1 + len(shards)),
            out_specs=pl.BlockSpec(memory_space=pltpu.VMEM),
            scratch_shapes=[
                pltpu.VMEM((len(shards), own_rows, share), BF16),
                pltpu.VMEM(adjacency.shape, BF16),
                pltpu.SemaphoreType.DMA((len(shards) + 1,)),
            ],
            compiler_params=pltpu.CompilerParams(vmem_limit_bytes=VMEM_BYTES),
            cost_estimate=pl.CostEstimate(
                flops=2 * slots * block * block * share,
                bytes_accessed=2 * own_rows * blk_count * share,
                transcendentals=0,
            ),
        )(slot_at, panel_at, adjacency, *shards)

    def exchange(value):
        parts = value.reshape(row_count, 2 * block, share)
        return lax.all_to_all(parts, "rows", 0, 0, tiled=True).reshape(slots, block, share)

    columns = [slice(k * share, (k + 1) * share) for k in range(CHUNKS)]
    terms = [exchange(forward(gather(hidden[:, cols]))) for cols in columns]

    output, *sends, local_grad = pl.pallas_call(
        owner_kernel,
        out_shape=(
            jax.ShapeDtypeStruct((own_rows, width), BF16),
            *[jax.ShapeDtypeStruct((slots, block, share), BF16)] * CHUNKS,
            jax.ShapeDtypeStruct((width, width), F32),
        ),
        in_specs=smem(1) + vmem(CHUNKS + 2),
        out_specs=tuple(vmem(CHUNKS + 2)),
        scratch_shapes=[pltpu.VMEM((own_rows, width), F32)],
        compiler_params=pltpu.CompilerParams(vmem_limit_bytes=VMEM_BYTES),
        cost_estimate=pl.CostEstimate(
            flops=4 * own_rows * width * width,
            bytes_accessed=12 * own_rows * width,
            transcendentals=own_rows * width,
        ),
    )(local_got, *terms, weight, marked)

    def backward(got):
        far_got = move(got, 0, 0, 1)
        return pl.pallas_call(
            backward_kernel,
            out_shape=[jax.ShapeDtypeStruct((own_rows, share), BF16)] * 8,
            in_specs=smem(2) + vmem(4),
            out_specs=vmem(8),
            scratch_shapes=[pltpu.VMEM((8 * own_blocks, block, share), F32)],
            compiler_params=pltpu.CompilerParams(vmem_limit_bytes=VMEM_BYTES),
            cost_estimate=pl.CostEstimate(
                flops=2 * slots * block * block * share,
                bytes_accessed=2 * own_rows * blk_count * share,
                transcendentals=0,
            ),
        )(slot_both, place_both, adjacency, far_tiles, got, far_got)

    def scatter(parts):
        own, plus, twice, minus, across, across_plus, across_twice, across_minus = parts
        wide = lambda value: value.astype(F32)
        from_minus = move(across_plus, 1, 0, 0)
        from_plus = move(across_minus, -1, 0, 0)
        from_across = move(across_twice, 0, 1, 0)
        across = (wide(across) + wide(from_minus) + wide(from_plus)).astype(BF16)
        twice = (wide(twice) + wide(from_across)).astype(BF16)
        got = [move(plus, 1, 0, 0), move(minus, -1, 0, 0), move(across, 0, 1, 0), move(twice, 2, 0, 0)]
        return sum([wide(value) for value in got], wide(own)).astype(BF16)

    d_proj = [scatter(backward(exchange(send))) for send in sends]
    d_hidden = sum(
        lax.dot_general(
            part, weight[:, cols], (((1,), (1,)), ((), ())), preferred_element_type=F32
        )
        for part, cols in zip(d_proj, columns)
    ).astype(BF16)

    pieces = local_grad.reshape(blk_count, width // blk_count, width)
    piece = jnp.sum(lax.all_to_all(pieces, "blk", 0, 0, tiled=True), axis=0)
    copies = jnp.broadcast_to(piece[None], (row_count, *piece.shape))
    piece = jnp.sum(lax.all_to_all(copies, "rows", 0, 0, tiled=True), axis=0)
    copies = jnp.broadcast_to(piece[None], (blk_count, *piece.shape))
    node_total = own_rows * row_count * blk_count
    d_weight = lax.all_to_all(copies, "blk", 0, 0, tiled=True).reshape(width, width)
    return (output, d_hidden, d_weight * (1.0 / math.sqrt(node_total)))


def solution(mesh):
    both = ("rows", "blk")
    return jax.shard_map(
        body,
        mesh=mesh,
        in_specs=(P(both, None), P(), P(both, None, None), P(both), P(both), P(both, None), P(both)),
        out_specs=(P(both, None), P(both, None), P()),
        check_vma=False,
    )
```

```python
import math

import jax
import jax.numpy as jnp
from jax import lax
from jax.experimental import pallas as pl
from jax.experimental.pallas import tpu as pltpu
from jax.sharding import PartitionSpec as P

BF16 = jnp.bfloat16
F32 = jnp.float32
CHUNKS = 2
NOTE = 16
GROUP = 8
VMEM_BYTES = 56 * 1024 * 1024
SMEM_SPEC = pl.BlockSpec(memory_space=pltpu.SMEM)
VMEM_SPEC = pl.BlockSpec(memory_space=pltpu.VMEM)
ANY_SPEC = pl.BlockSpec(memory_space=pl.ANY)
PARAMS = pltpu.CompilerParams(vmem_limit_bytes=VMEM_BYTES)


def after(value, *others):
    return lax.optimization_barrier((value, *others))[0]


def blk_pairs(blk_count, dx, dy, dc):
    x_count = blk_count // 4
    pairs = []
    for b in range(blk_count):
        x, y, c = b // 4, (b // 2) % 2, b % 2
        pairs.append((b, ((x + dx) % x_count) * 4 + ((y + dy) % 2) * 2 + (c + dc) % 2))
    return pairs


def run_all(copies):
    for copy in copies:
        copy.start()
    for copy in copies:
        copy.wait()


def forward_kernel(chunk, slot_ref, source_ref, local_ref, tiles_ref, *refs):
    shards, out_ref, (held, tiles, sems) = refs[:-4], refs[-4], refs[-3:]
    copies = [pltpu.make_async_copy(tiles_ref, tiles, sems.at[len(shards)])]
    share = held.shape[2]
    for k, shard in enumerate(shards):
        part = shard if shard.shape[1] == share else shard.at[:, pl.ds(chunk * share, share)]
        copies.append(pltpu.make_async_copy(part, held.at[k], sems.at[k]))
    run_all(copies)
    block = tiles.shape[1]
    noted = out_ref.shape[1] > 2 * block
    for s in range(2 * out_ref.shape[0]):
        slot = jnp.maximum(slot_ref[s], 0)
        source = jnp.maximum(source_ref[s], 0)
        panel = held[source // 8, pl.ds(pl.multiple_of((source % 8) * block, block), block), :]
        product = jnp.dot(tiles[slot], panel, preferred_element_type=F32)
        out_ref[s // 2, (s % 2) * block : (s % 2 + 1) * block, :] = product.astype(BF16)
    if noted:
        row = lax.broadcasted_iota(jnp.int32, (NOTE, out_ref.shape[2]), 0)
        for p in range(out_ref.shape[0]):
            note = jnp.where(row == 0, local_ref[2 * p], local_ref[2 * p + 1])
            out_ref[p, 2 * block :, :] = note.astype(F32).astype(BF16)


def sum_terms(local_ref, term_ref, total, block):
    total[...] = jnp.zeros(total.shape, F32)

    def add(p, carry):
        for j in range(2):
            local = local_ref[2 * p + j]

            @pl.when(local >= 0)
            def _():
                rows = pl.ds(pl.multiple_of(local * block, block), block)
                total[rows, :] += term_ref[p, j * block : (j + 1) * block, :].astype(F32)

        return carry

    lax.fori_loop(0, term_ref.shape[0], add, 0)


def sum_kernel(block, local_ref, term_ref, out_ref, total):
    sum_terms(local_ref, term_ref, total, block)
    out_ref[...] = total[...].astype(BF16)


def owner_kernel(block, local_ref, term_ref, *refs):
    early, (weight_ref, up_ref, out_ref) = refs[: CHUNKS - 1], refs[CHUNKS - 1 : CHUNKS + 2]
    send_refs, (dw_ref, total, held) = refs[CHUNKS + 2 : -3], refs[-3:]
    width = term_ref.shape[2]
    sum_terms(local_ref, term_ref, total, block)
    weight = weight_ref[...]
    dw = jnp.zeros(dw_ref.shape, F32)
    for g in range(total.shape[0] // block):
        rows = slice(g * block, (g + 1) * block)
        parts = [ref[rows, :] for ref in early] + [total[rows, :].astype(BF16)]
        aggregated = jnp.concatenate(parts, axis=1)
        summed = jnp.dot(aggregated, weight, preferred_element_type=F32)
        logistic = jax.nn.sigmoid(summed)
        out_ref[rows, :] = (summed * logistic).astype(BF16)
        slope = logistic * (1.0 + summed * (1.0 - logistic))
        grad = (up_ref[rows, :].astype(F32) * slope).astype(BF16)
        held[rows, :] = grad
        dw = dw + lax.dot_general(
            aggregated, grad, (((0,), (0,)), ((), ())), preferred_element_type=F32
        )
    dw_ref[...] = dw

    for p in range(term_ref.shape[0]):
        for j in range(2):
            local = jnp.maximum(local_ref[2 * p + j], 0)
            rows = pl.ds(pl.multiple_of(local * block, block), block)
            for k, send in enumerate(send_refs):
                send[p, j * block : (j + 1) * block, :] = held[rows, k * width : (k + 1) * width]


def backward_kernel(block, count_ref, tile_ref, grad_ref, place_ref, tiles_ref, near_ref, far_ref, *refs):
    outs, (tiles, grads, held, sems) = refs[:-4], refs[-4:]
    half = near_ref.shape[0]
    loads = [
        pltpu.make_async_copy(tiles_ref, tiles, sems.at[0]),
        pltpu.make_async_copy(near_ref.at[:, pl.ds(0, 2 * block)], grads.at[pl.ds(0, half)], sems.at[1]),
        pltpu.make_async_copy(far_ref, grads.at[pl.ds(half, half)], sems.at[2]),
    ]
    for load in loads:
        load.start()
    held[...] = jnp.zeros(held.shape, F32)
    for load in loads:
        load.wait()

    def group(i, carry):
        entries = [i * GROUP + u for u in range(GROUP)]
        products = [
            jnp.dot(
                tiles[tile_ref[e]],
                grads[grad_ref[e] // 2, pl.ds(pl.multiple_of(grad_ref[e] % 2 * block, block), block), :],
                preferred_element_type=F32,
            )
            for e in entries
        ]
        for e, product in zip(entries, products):
            held[pl.ds(pl.multiple_of(place_ref[e] * block, block), block), :] += product
        return carry

    lax.fori_loop(0, (count_ref[0] + GROUP - 1) // GROUP, group, 0)
    rows = outs[0].shape[0]
    for k, out in enumerate(outs):
        out[...] = held[k * rows : (k + 1) * rows, :].astype(BF16)


def body(hidden, weight, adjacency, tile_target, tile_source, upstream, labels):
    block = adjacency.shape[1]
    slots = adjacency.shape[0]
    own_rows, width = hidden.shape
    own_blocks = own_rows // block
    row_count = lax.axis_size("rows")
    blk_count = lax.axis_size("blk")
    share = width // CHUNKS
    me = lax.axis_index("blk")
    columns = [slice(k * share, (k + 1) * share) for k in range(CHUNKS)]

    def move(value, dx, dy, dc):
        return lax.ppermute(value, "blk", blk_pairs(blk_count, dx, dy, dc))

    order = jnp.arange(slots, dtype=jnp.int32)
    peer = tile_target // own_blocks
    earlier = (peer[:, None] == peer[None, :]) & (order[None, :] < order[:, None])
    rank = jnp.sum(earlier.astype(jnp.int32), axis=1)
    spot = jnp.where(peer < row_count, peer * 2 + rank, -1)
    at = (spot[:, None] == order[None, :]).astype(jnp.int32)
    slot_at = jnp.sum(at * (order[:, None] + 1), axis=0) - 1
    local_at = jnp.sum(at * (tile_target[:, None] % own_blocks + 1), axis=0) - 1
    source_at = jnp.sum(at * (tile_source[:, None] + 1), axis=0) - 1
    holder = source_at // own_blocks
    dx = (holder // 4 - me // 4) % 4
    dy = (holder // 2 - me // 2) % 2
    dc = (holder - me) % 2
    inner = (dy * 4 + dx) * own_blocks + source_at % own_blocks
    places = 8 * own_blocks
    panel_at = jnp.where(source_at >= 0, dc * places + inner, -1)
    near_place = jnp.where((source_at >= 0) & (dc == 0), inner, places)
    cross_place = jnp.where((source_at >= 0) & (dc == 1), inner, places)

    far = move(jnp.stack([slot_at, cross_place]), 0, 0, 1)
    tile_of = jnp.concatenate([jnp.maximum(slot_at, 0), jnp.maximum(far[0], 0) + slots])
    place_of = jnp.concatenate([near_place, far[1]])
    used = (place_of < places).astype(jnp.int32)
    count = jnp.sum(used).reshape(1)
    entry = jnp.arange(2 * slots, dtype=jnp.int32)
    before = (entry[None, :] < entry[:, None]).astype(jnp.int32)
    used_before = jnp.sum(before * used[None, :], axis=1)
    position = jnp.where(used > 0, used_before, count + entry - used_before)
    chosen = (position[:, None] == entry[None, :]).astype(jnp.int32)
    tile_list = jnp.sum(chosen * tile_of[:, None], axis=0)
    grad_list = jnp.sum(chosen * entry[:, None], axis=0)
    place_list = jnp.sum(chosen * place_of[:, None], axis=0)

    turned = jnp.swapaxes(adjacency, 1, 2)
    all_turned = jnp.concatenate([turned, move(turned, 0, 0, 1)])
    marked = upstream * labels.astype(BF16)[:, None]

    def forward(chunk, shards, note):
        return pl.pallas_call(
            lambda *refs: forward_kernel(chunk, *refs),
            out_shape=jax.ShapeDtypeStruct((row_count, 2 * block + note, share), BF16),
            in_specs=[SMEM_SPEC] * 3 + [ANY_SPEC] * (1 + len(shards)),
            out_specs=VMEM_SPEC,
            scratch_shapes=[
                pltpu.VMEM((len(shards), own_rows, share), BF16),
                pltpu.VMEM(adjacency.shape, BF16),
                pltpu.SemaphoreType.DMA((len(shards) + 1,)),
            ],
            compiler_params=PARAMS,
            cost_estimate=pl.CostEstimate(
                flops=2 * slots * block * block * share,
                bytes_accessed=2 * own_rows * blk_count * share,
                transcendentals=0,
            ),
        )(slot_at, panel_at, local_at, adjacency, *shards)

    def exchange(value):
        return lax.all_to_all(value, "rows", 0, 0, tiled=True)

    def first_round(own):
        return [move(own, -1, 0, 0), move(own, 1, 0, 0), move(own, 0, 1, 0), move(own, 2, 0, 0)]

    def second_round(own, received):
        plus, minus, across, twice = received
        near = [own, plus, twice, minus, across]
        near += [move(across, -1, 0, 0), move(twice, 0, 1, 0), move(across, 1, 0, 0)]
        return near + [move(value, 0, 0, 1) for value in near]

    owns = [hidden[:, cols] for cols in columns]
    rounds = [first_round(owns[0])]
    owns[1] = after(owns[1], *rounds[0])
    rounds.append(first_round(owns[1]))
    sums = forward(0, second_round(owns[0], rounds[0]), NOTE)
    got = [exchange(after(sums, *rounds[1]))]
    got.append(exchange(forward(1, second_round(owns[1], rounds[1]), 0)))
    local_got = got[0][:, 2 * block : 2 * block + 2, 0].astype(jnp.int32).reshape(-1)

    early = [
        pl.pallas_call(
            lambda *refs: sum_kernel(block, *refs),
            out_shape=jax.ShapeDtypeStruct((own_rows, share), BF16),
            in_specs=[SMEM_SPEC, VMEM_SPEC],
            out_specs=VMEM_SPEC,
            scratch_shapes=[pltpu.VMEM((own_rows, share), F32)],
            compiler_params=PARAMS,
            cost_estimate=pl.CostEstimate(
                flops=slots * block * share, bytes_accessed=2 * slots * block * share, transcendentals=0
            ),
        )(local_got, term)
        for term in got[:-1]
    ]
    tail_rows = width // blk_count * CHUNKS
    output, *sends, local_grad = pl.pallas_call(
        lambda *refs: owner_kernel(block, *refs),
        out_shape=(
            jax.ShapeDtypeStruct((own_rows, width), BF16),
            *[
                jax.ShapeDtypeStruct((row_count, 2 * block + tail, share), BF16)
                for tail in [0] * (CHUNKS - 1) + [tail_rows]
            ],
            jax.ShapeDtypeStruct((width, width), F32),
        ),
        in_specs=[SMEM_SPEC] + [VMEM_SPEC] * (CHUNKS + 2),
        out_specs=(VMEM_SPEC,) * (CHUNKS + 2),
        scratch_shapes=[pltpu.VMEM((own_rows, share), F32), pltpu.VMEM((own_rows, width), BF16)],
        compiler_params=PARAMS,
        cost_estimate=pl.CostEstimate(
            flops=4 * own_rows * width * width,
            bytes_accessed=12 * own_rows * width,
            transcendentals=own_rows * width,
        ),
    )(local_got, got[-1], *early, weight, marked)

    def backward(near):
        far_near = move(near[:, : 2 * block, :], 0, 0, 1)
        return pl.pallas_call(
            lambda *refs: backward_kernel(block, *refs),
            out_shape=[jax.ShapeDtypeStruct((own_rows, share), BF16)] * 8,
            in_specs=[SMEM_SPEC] * 4 + [ANY_SPEC] * 3,
            out_specs=[VMEM_SPEC] * 8,
            scratch_shapes=[
                pltpu.VMEM((2 * slots, block, block), BF16),
                pltpu.VMEM((2 * row_count, 2 * block, share), BF16),
                pltpu.VMEM(((places + 1) * block, share), F32),
                pltpu.SemaphoreType.DMA((3,)),
            ],
            compiler_params=PARAMS,
            cost_estimate=pl.CostEstimate(
                flops=2 * slots * block * block * share,
                bytes_accessed=2 * own_rows * blk_count * share,
                transcendentals=0,
            ),
        )(count, tile_list, grad_list, place_list, all_turned, near, far_near)

    def wide_sum(*values):
        return sum(value.astype(F32) for value in values).astype(BF16)

    def first_sums(parts):
        own, plus, twice, minus, across, across_plus, across_twice, across_minus = parts
        from_minus = move(across_plus, 1, 0, 0)
        from_plus = move(across_minus, -1, 0, 0)
        from_across = move(across_twice, 0, 1, 0)
        return [
            own, plus, minus, wide_sum(across, from_minus, from_plus), wide_sum(twice, from_across)
        ]

    def last_sum(parts):
        own, plus, minus, across, twice = parts
        return wide_sum(
            own, move(plus, 1, 0, 0), move(minus, -1, 0, 0), move(across, 0, 1, 0), move(twice, 2, 0, 0)
        )

    x, y, c = me // 4, (me // 2) % 2, me % 2

    def halve(value, bit, dy, dc):
        half = value.shape[0] // 2
        keep = lax.dynamic_slice_in_dim(value, bit * half, half)
        return keep + move(lax.dynamic_slice_in_dim(value, (1 - bit) * half, half), 0, dy, dc)

    value = halve(halve(local_grad, c, 0, 1), y, 1, 0)
    rows = value.shape[0] // 4
    terms = [lax.dynamic_slice_in_dim(value, ((x + step) % 4) * rows, rows) for step in range(4)]
    piece = terms[0] + sum(move(terms[step], step, 0, 0) for step in (1, 2, 3))
    piece = jnp.concatenate([piece[:, cols] for cols in columns]).astype(BF16)
    sends[-1] = sends[-1].at[:, 2 * block :, :].set(piece[None])

    back = [exchange(sends[0])]
    back.append(exchange(after(sends[1], back[0])))
    piece = jnp.sum(back[-1][:, 2 * block :, :].astype(F32), axis=0)
    half_way = first_sums(backward(back[0]))
    d_proj = [last_sum(half_way)]
    d_proj.append(last_sum(first_sums(backward(after(back[1], *half_way[3:])))))
    d_hidden = sum(
        lax.dot_general(
            part, weight[:, cols], (((1,), (1,)), ((), ())), preferred_element_type=F32
        )
        for part, cols in zip(d_proj, columns)
    ).astype(BF16)

    pieces = lax.all_to_all(
        jnp.broadcast_to(piece[None], (blk_count, *piece.shape)), "blk", 0, 0, tiled=True
    )
    pieces = pieces.reshape(4, 2, 2, CHUNKS, rows, share).transpose(2, 1, 0, 4, 3, 5)
    node_total = own_rows * row_count * blk_count
    d_weight = pieces.reshape(width, width) * (1.0 / math.sqrt(node_total))
    return (output, d_hidden, d_weight)


def solution(mesh):
    both = ("rows", "blk")
    return jax.shard_map(
        body,
        mesh=mesh,
        in_specs=(P(both, None), P(), P(both, None, None), P(both), P(both), P(both, None), P(both)),
        out_specs=(P(both, None), P(both, None), P()),
        check_vma=False,
    )
```

```python
import math

import jax
import jax.numpy as jnp
from jax import lax
from jax.experimental import pallas as pl
from jax.experimental.pallas import tpu as pltpu
from jax.sharding import PartitionSpec as P

BF16 = jnp.bfloat16
F32 = jnp.float32
CHUNKS = 2
NOTE = 16
GROUP = 8
VMEM_BYTES = 56 * 1024 * 1024
SMEM_SPEC = pl.BlockSpec(memory_space=pltpu.SMEM)
VMEM_SPEC = pl.BlockSpec(memory_space=pltpu.VMEM)
ANY_SPEC = pl.BlockSpec(memory_space=pl.ANY)
PARAMS = pltpu.CompilerParams(vmem_limit_bytes=VMEM_BYTES)


def after(value, *others):
    return lax.optimization_barrier((value, *others))[0]


def blk_pairs(blk_count, dx, dy, dc):
    x_count = blk_count // 4
    pairs = []
    for b in range(blk_count):
        x, y, c = b // 4, (b // 2) % 2, b % 2
        pairs.append((b, ((x + dx) % x_count) * 4 + ((y + dy) % 2) * 2 + (c + dc) % 2))
    return pairs


def run_all(copies):
    for copy in copies:
        copy.start()
    for copy in copies:
        copy.wait()


def forward_kernel(slot_ref, source_ref, local_ref, tiles_ref, *refs):
    shards, out_ref, (held, tiles, sems) = refs[:-4], refs[-4], refs[-3:]
    rows = held.shape[1]
    copies = [pltpu.make_async_copy(tiles_ref, tiles, sems.at[0])]
    side = len(shards) // 2
    for core in range(2):
        own, across, twice, across_twice, plus, minus = shards[core * side : (core + 1) * side]
        parts = [
            own, plus.at[pl.ds(0, rows)], twice, minus.at[pl.ds(0, rows)],
            across, plus.at[pl.ds(rows, rows)],
            across_twice, minus.at[pl.ds(rows, rows)],
        ]
        for part in parts:
            place = len(copies) - 1
            copies.append(pltpu.make_async_copy(part, held.at[place], sems.at[place + 1]))
    run_all(copies)
    block = tiles.shape[1]
    noted = out_ref.shape[1] > 2 * block
    for s in range(2 * out_ref.shape[0]):
        slot = jnp.maximum(slot_ref[s], 0)
        source = jnp.maximum(source_ref[s], 0)
        panel = held[source // 8, pl.ds(pl.multiple_of((source % 8) * block, block), block), :]
        product = jnp.dot(tiles[slot], panel, preferred_element_type=F32)
        out_ref[s // 2, (s % 2) * block : (s % 2 + 1) * block, :] = product.astype(BF16)
    if noted:
        row = lax.broadcasted_iota(jnp.int32, (NOTE, out_ref.shape[2]), 0)
        for p in range(out_ref.shape[0]):
            note = jnp.where(row == 0, local_ref[2 * p], local_ref[2 * p + 1])
            out_ref[p, 2 * block :, :] = note.astype(F32).astype(BF16)


def sum_terms(local_ref, term_ref, total, block):
    total[...] = jnp.zeros(total.shape, F32)

    def add(p, carry):
        for j in range(2):
            local = local_ref[2 * p + j]

            @pl.when(local >= 0)
            def _():
                rows = pl.ds(pl.multiple_of(local * block, block), block)
                total[rows, :] += term_ref[p, j * block : (j + 1) * block, :].astype(F32)

        return carry

    lax.fori_loop(0, term_ref.shape[0], add, 0)


def sum_kernel(block, local_ref, term_ref, out_ref, total):
    sum_terms(local_ref, term_ref, total, block)
    out_ref[...] = total[...].astype(BF16)


def owner_kernel(block, local_ref, term_ref, *refs):
    early, (weight_ref, up_ref), (sum_ref, grad_ref, send_ref, total) = (
        refs[: CHUNKS - 1],
        refs[CHUNKS - 1 : CHUNKS + 1],
        refs[CHUNKS + 1 :],
    )
    sum_terms(local_ref, term_ref, total, block)
    weight = weight_ref[...]
    for g in range(total.shape[0] // block):
        rows = slice(g * block, (g + 1) * block)
        last = total[rows, :].astype(BF16)
        sum_ref[rows, :] = last
        summed = jnp.dot(
            jnp.concatenate([ref[rows, :] for ref in early] + [last], axis=1),
            weight,
            preferred_element_type=F32,
        )
        logistic = jax.nn.sigmoid(summed)
        slope = logistic * (1.0 + summed * (1.0 - logistic))
        grad_ref[rows, :] = (up_ref[rows, :].astype(F32) * slope).astype(BF16)
    lay_out(local_ref, grad_ref, send_ref, 0, block)


def lay_out(local_ref, grad_ref, send_ref, chunk, block):
    width = send_ref.shape[2]
    cols = slice(chunk * width, (chunk + 1) * width)
    for p in range(send_ref.shape[0]):
        for j in range(2):
            local = jnp.maximum(local_ref[2 * p + j], 0)
            rows = pl.ds(pl.multiple_of(local * block, block), block)
            send_ref[p, j * block : (j + 1) * block, :] = grad_ref[rows, cols]


def finish_kernel(block, local_ref, *refs):
    parts, (grad_ref, weight_ref, out_ref), (*send_refs, dw_ref) = (
        refs[:CHUNKS],
        refs[CHUNKS : CHUNKS + 3],
        refs[CHUNKS + 3 :],
    )
    for k, send_ref in enumerate(send_refs):
        lay_out(local_ref, grad_ref, send_ref, k + 1, block)
    weight = weight_ref[...]
    dw = jnp.zeros(dw_ref.shape, F32)
    for g in range(out_ref.shape[0] // block):
        rows = slice(g * block, (g + 1) * block)
        aggregated = jnp.concatenate([ref[rows, :] for ref in parts], axis=1)
        summed = jnp.dot(aggregated, weight, preferred_element_type=F32)
        out_ref[rows, :] = (summed * jax.nn.sigmoid(summed)).astype(BF16)
        dw = dw + lax.dot_general(
            aggregated, grad_ref[rows, :], (((0,), (0,)), ((), ())), preferred_element_type=F32
        )
    dw_ref[...] = dw


def backward_kernel(block, count_ref, tile_ref, grad_ref, place_ref, tiles_ref, near_ref, far_ref, *refs):
    outs, (tiles, grads, held, sems) = refs[:-4], refs[-4:]
    half = near_ref.shape[0]
    loads = [
        pltpu.make_async_copy(tiles_ref, tiles, sems.at[0]),
        pltpu.make_async_copy(near_ref.at[:, pl.ds(0, 2 * block)], grads.at[pl.ds(0, half)], sems.at[1]),
        pltpu.make_async_copy(far_ref, grads.at[pl.ds(half, half)], sems.at[2]),
    ]
    for load in loads:
        load.start()
    held[...] = jnp.zeros(held.shape, F32)
    for load in loads:
        load.wait()

    def group(i, carry):
        entries = [i * GROUP + u for u in range(GROUP)]
        products = [
            jnp.dot(
                tiles[tile_ref[e]],
                grads[grad_ref[e] // 2, pl.ds(pl.multiple_of(grad_ref[e] % 2 * block, block), block), :],
                preferred_element_type=F32,
            )
            for e in entries
        ]
        for e, product in zip(entries, products):
            held[pl.ds(pl.multiple_of(place_ref[e] * block, block), block), :] += product
        return carry

    lax.fori_loop(0, (count_ref[0] + GROUP - 1) // GROUP, group, 0)
    own, across, twice, across_twice, plus, minus = outs
    rows = own.shape[0]
    order = [
        own, plus.at[pl.ds(0, rows)], twice, minus.at[pl.ds(0, rows)],
        across, plus.at[pl.ds(rows, rows)], across_twice, minus.at[pl.ds(rows, rows)],
    ]
    for k, out in enumerate(order):
        out[...] = held[k * rows : (k + 1) * rows, :].astype(BF16)


def body(hidden, weight, adjacency, tile_target, tile_source, upstream, labels):
    block = adjacency.shape[1]
    slots = adjacency.shape[0]
    own_rows, width = hidden.shape
    own_blocks = own_rows // block
    row_count = lax.axis_size("rows")
    blk_count = lax.axis_size("blk")
    share = width // CHUNKS
    me = lax.axis_index("blk")
    columns = [slice(k * share, (k + 1) * share) for k in range(CHUNKS)]

    def move(value, dx, dy, dc):
        return lax.ppermute(value, "blk", blk_pairs(blk_count, dx, dy, dc))

    order = jnp.arange(slots, dtype=jnp.int32)
    peer = tile_target // own_blocks
    earlier = (peer[:, None] == peer[None, :]) & (order[None, :] < order[:, None])
    rank = jnp.sum(earlier.astype(jnp.int32), axis=1)
    spot = jnp.where(peer < row_count, peer * 2 + rank, -1)
    at = (spot[:, None] == order[None, :]).astype(jnp.int32)
    slot_at = jnp.sum(at * (order[:, None] + 1), axis=0) - 1
    local_at = jnp.sum(at * (tile_target[:, None] % own_blocks + 1), axis=0) - 1
    source_at = jnp.sum(at * (tile_source[:, None] + 1), axis=0) - 1
    holder = source_at // own_blocks
    dx = (holder // 4 - me // 4) % 4
    dy = (holder // 2 - me // 2) % 2
    dc = (holder - me) % 2
    inner = (dy * 4 + dx) * own_blocks + source_at % own_blocks
    places = 8 * own_blocks
    panel_at = jnp.where(source_at >= 0, dc * places + inner, -1)
    near_place = jnp.where((source_at >= 0) & (dc == 0), inner, places)
    cross_place = jnp.where((source_at >= 0) & (dc == 1), inner, places)

    far = move(jnp.stack([slot_at, cross_place]), 0, 0, 1)
    tile_of = jnp.concatenate([jnp.maximum(slot_at, 0), jnp.maximum(far[0], 0) + slots])
    place_of = jnp.concatenate([near_place, far[1]])
    used = (place_of < places).astype(jnp.int32)
    used_count = jnp.sum(used).reshape(1)
    entry = jnp.arange(2 * slots, dtype=jnp.int32)
    before = (entry[None, :] < entry[:, None]).astype(jnp.int32)
    used_before = jnp.sum(before * used[None, :], axis=1)
    position = jnp.where(used > 0, used_before, used_count + entry - used_before)
    chosen = (position[:, None] == entry[None, :]).astype(jnp.int32)
    tile_list = jnp.sum(chosen * tile_of[:, None], axis=0)
    grad_list = jnp.sum(chosen * entry[:, None], axis=0)
    place_list = jnp.sum(chosen * place_of[:, None], axis=0)

    turned = jnp.swapaxes(adjacency, 1, 2)
    all_turned = jnp.concatenate([turned, move(turned, 0, 0, 1)])
    marked = after(
        upstream * labels.astype(BF16)[:, None], all_turned, tile_list, grad_list, place_list, used_count
    )

    def forward(shards, note):
        return pl.pallas_call(
            forward_kernel,
            out_shape=jax.ShapeDtypeStruct((row_count, 2 * block + note, share), BF16),
            in_specs=[SMEM_SPEC] * 3 + [ANY_SPEC] * (1 + len(shards)),
            out_specs=VMEM_SPEC,
            scratch_shapes=[
                pltpu.VMEM((blk_count, own_rows, share), BF16),
                pltpu.VMEM(adjacency.shape, BF16),
                pltpu.SemaphoreType.DMA((blk_count + 1,)),
            ],
            compiler_params=PARAMS,
            cost_estimate=pl.CostEstimate(
                flops=2 * slots * block * block * share,
                bytes_accessed=2 * own_rows * blk_count * share,
                transcendentals=0,
            ),
        )(slot_at, panel_at, local_at, adjacency, *shards)

    def exchange(value):
        return lax.all_to_all(value, "rows", 0, 0, tiled=True)

    gathered, pairs = [], []
    for cols in columns:
        own = after(hidden[:, cols], *pairs)
        twice, across = move(own, 2, 0, 0), move(own, 0, 1, 0)
        pair = after(jnp.concatenate([own, across]), twice, slot_at, panel_at, local_at)
        pairs = [move(pair, -1, 0, 0), move(pair, 1, 0, 0)]
        near = [own, across, twice, move(twice, 0, 1, 0), *pairs]
        gathered.append(near + [move(value, 0, 0, 1) for value in near])
    sums = forward(gathered[0], NOTE)
    got = [exchange(after(sums, *gathered[1][1:3])), exchange(forward(gathered[1], 0))]
    local_got = got[0][:, 2 * block : 2 * block + 2, 0].astype(jnp.int32).reshape(-1)

    early = [
        pl.pallas_call(
            lambda *refs: sum_kernel(block, *refs),
            out_shape=jax.ShapeDtypeStruct((own_rows, share), BF16),
            in_specs=[SMEM_SPEC, VMEM_SPEC],
            out_specs=VMEM_SPEC,
            scratch_shapes=[pltpu.VMEM((own_rows, share), F32)],
            compiler_params=PARAMS,
            cost_estimate=pl.CostEstimate(
                flops=slots * block * share, bytes_accessed=2 * slots * block * share, transcendentals=0
            ),
        )(local_got, term)
        for term in got[:-1]
    ]
    last_sums, grad, send = pl.pallas_call(
        lambda *refs: owner_kernel(block, *refs),
        out_shape=(
            jax.ShapeDtypeStruct((own_rows, share), BF16),
            jax.ShapeDtypeStruct((own_rows, width), BF16),
            jax.ShapeDtypeStruct((row_count, 2 * block, share), BF16),
        ),
        in_specs=[SMEM_SPEC] + [VMEM_SPEC] * (CHUNKS + 2),
        out_specs=(VMEM_SPEC,) * 3,
        scratch_shapes=[pltpu.VMEM((own_rows, share), F32)],
        compiler_params=PARAMS,
        cost_estimate=pl.CostEstimate(
            flops=2 * own_rows * width * width,
            bytes_accessed=10 * own_rows * width,
            transcendentals=own_rows * width,
        ),
    )(local_got, got[-1], *early, weight, marked)
    back = [exchange(send)]
    tail_rows = width // blk_count * CHUNKS
    output, *sends, local_grad = pl.pallas_call(
        lambda *refs: finish_kernel(block, *refs),
        out_shape=(
            jax.ShapeDtypeStruct((own_rows, width), BF16),
            *[
                jax.ShapeDtypeStruct((row_count, 2 * block + tail, share), BF16)
                for tail in [0] * (CHUNKS - 2) + [tail_rows]
            ],
            jax.ShapeDtypeStruct((width, width), F32),
        ),
        in_specs=[SMEM_SPEC] + [VMEM_SPEC] * (CHUNKS + 2),
        out_specs=(VMEM_SPEC,) * (CHUNKS + 1),
        compiler_params=PARAMS,
        cost_estimate=pl.CostEstimate(
            flops=4 * own_rows * width * width,
            bytes_accessed=8 * own_rows * width,
            transcendentals=own_rows * width,
        ),
    )(local_got, *early, last_sums, grad, weight)

    def backward(near):
        far_near = move(near[:, : 2 * block, :], 0, 0, 1)
        return pl.pallas_call(
            lambda *refs: backward_kernel(block, *refs),
            out_shape=[
                jax.ShapeDtypeStruct((count * own_rows, share), BF16) for count in (1, 1, 1, 1, 2, 2)
            ],
            in_specs=[SMEM_SPEC] * 4 + [ANY_SPEC] * 3,
            out_specs=[VMEM_SPEC] * 6,
            scratch_shapes=[
                pltpu.VMEM((2 * slots, block, block), BF16),
                pltpu.VMEM((2 * row_count, 2 * block, share), BF16),
                pltpu.VMEM(((places + 1) * block, share), F32),
                pltpu.SemaphoreType.DMA((3,)),
            ],
            compiler_params=PARAMS,
            cost_estimate=pl.CostEstimate(
                flops=2 * slots * block * block * share,
                bytes_accessed=2 * own_rows * blk_count * share,
                transcendentals=0,
            ),
        )(used_count, tile_list, grad_list, place_list, all_turned, near, far_near)

    def wide_sum(*values):
        return sum(value.astype(F32) for value in values).astype(BF16)

    def first_sums(parts):
        own, across, twice, across_twice, plus, minus = parts
        from_minus, from_plus = move(plus, 1, 0, 0), move(minus, -1, 0, 0)
        twice = wide_sum(twice, move(across_twice, 0, 1, 0))
        own = wide_sum(own, from_minus[:own_rows], from_plus[:own_rows])
        across = wide_sum(across, from_minus[own_rows:], from_plus[own_rows:])
        return [own, across, twice]

    def last_moves(parts):
        own, across, twice = parts
        return [own, move(across, 0, 1, 0), move(twice, 2, 0, 0)]

    x, y, c = me // 4, (me // 2) % 2, me % 2

    def halve(value, bit, dy, dc):
        half = value.shape[0] // 2
        keep = lax.dynamic_slice_in_dim(value, bit * half, half)
        return keep + move(lax.dynamic_slice_in_dim(value, (1 - bit) * half, half), 0, dy, dc)

    value = halve(halve(local_grad, c, 0, 1), y, 1, 0)
    rows = value.shape[0] // 4
    terms = [lax.dynamic_slice_in_dim(value, ((x + step) % 4) * rows, rows) for step in range(4)]
    piece = terms[0] + sum(move(terms[step], step, 0, 0) for step in (1, 2, 3))
    piece = jnp.concatenate([piece[:, cols] for cols in columns]).astype(BF16)
    sends[-1] = sends[-1].at[:, 2 * block :, :].set(piece[None])

    back.append(exchange(after(sends[-1], back[0])))
    piece = jnp.sum(back[-1][:, 2 * block :, :].astype(F32), axis=0)
    half_way = first_sums(backward(back[0]))
    last = backward(after(back[1], *half_way))
    received = last_moves(half_way)
    last_half_way = first_sums(after(tuple(last), *received))
    d_proj = [wide_sum(*received), wide_sum(*last_moves(last_half_way))]
    d_hidden = sum(
        lax.dot_general(
            part, weight[:, cols], (((1,), (1,)), ((), ())), preferred_element_type=F32
        )
        for part, cols in zip(d_proj, columns)
    ).astype(BF16)

    pieces = lax.all_to_all(
        jnp.broadcast_to(piece[None], (blk_count, *piece.shape)), "blk", 0, 0, tiled=True
    )
    pieces = pieces.reshape(4, 2, 2, CHUNKS, rows, share).transpose(2, 1, 0, 4, 3, 5)
    node_total = own_rows * row_count * blk_count
    d_weight = pieces.reshape(width, width) * (1.0 / math.sqrt(node_total))
    return (output, d_hidden, d_weight)


def solution(mesh):
    both = ("rows", "blk")
    return jax.shard_map(
        body,
        mesh=mesh,
        in_specs=(P(both, None), P(), P(both, None, None), P(both), P(both), P(both, None), P(both)),
        out_specs=(P(both, None), P(both, None), P()),
        check_vma=False,
    )
```

```python
import math

import jax
import jax.numpy as jnp
from jax import lax
from jax.experimental import pallas as pl
from jax.experimental.pallas import tpu as pltpu
from jax.sharding import PartitionSpec as P

BF16 = jnp.bfloat16
F32 = jnp.float32
CHUNKS = 2
NOTE = 16
GROUP = 4
SMEM_SPEC = pl.BlockSpec(memory_space=pltpu.SMEM)
VMEM_SPEC = pl.BlockSpec(memory_space=pltpu.VMEM)
ANY_SPEC = pl.BlockSpec(memory_space=pl.ANY)
HBM_SPEC = pl.BlockSpec(memory_space=pltpu.HBM)
MIB = 1024 * 1024
SMALL = pltpu.CompilerParams(vmem_limit_bytes=20 * MIB)
MIDDLE = pltpu.CompilerParams(vmem_limit_bytes=44 * MIB)
LARGE = pltpu.CompilerParams(vmem_limit_bytes=56 * MIB)


def after(value, *others):
    return lax.optimization_barrier((value, *others))[0]


def blk_pairs(blk_count, dx, dy, dc):
    x_count = blk_count // 4
    pairs = []
    for b in range(blk_count):
        x, y, c = b // 4, (b // 2) % 2, b % 2
        pairs.append((b, ((x + dx) % x_count) * 4 + ((y + dy) % 2) * 2 + (c + dc) % 2))
    return pairs


def run_all(copies):
    for copy in copies:
        copy.start()
    for copy in copies:
        copy.wait()


def forward_kernel(slot_ref, source_ref, local_ref, tiles_ref, *refs):
    shards, out_ref, (held, tiles, laid, sems, out_sems) = refs[:-6], refs[-6], refs[-5:]
    rows = held.shape[1]
    copies = [pltpu.make_async_copy(tiles_ref, tiles, sems.at[0])]
    side = len(shards) // 2
    for core in range(2):
        own, across, twice, across_twice, plus, minus = shards[core * side : (core + 1) * side]
        parts = [
            own, plus.at[pl.ds(0, rows)], twice, minus.at[pl.ds(0, rows)],
            across, plus.at[pl.ds(rows, rows)],
            across_twice, minus.at[pl.ds(rows, rows)],
        ]
        for part in parts:
            place = len(copies) - 1
            copies.append(pltpu.make_async_copy(part, held.at[place], sems.at[place + 1]))
    run_all(copies)
    block = tiles.shape[1]
    noted = out_ref.shape[1] > 2 * block
    row = lax.broadcasted_iota(jnp.int32, (NOTE, out_ref.shape[2]), 0)
    stores = []
    for p in range(out_ref.shape[0]):
        for j in range(2):
            slot = jnp.maximum(slot_ref[2 * p + j], 0)
            source = jnp.maximum(source_ref[2 * p + j], 0)
            panel = held[source // 8, pl.ds(pl.multiple_of((source % 8) * block, block), block), :]
            product = jnp.dot(tiles[slot], panel, preferred_element_type=F32)
            laid[p, j * block : (j + 1) * block, :] = product.astype(BF16)
        if noted:
            note = jnp.where(row == 0, local_ref[2 * p], local_ref[2 * p + 1])
            laid[p, 2 * block :, :] = note.astype(F32).astype(BF16)
        stores.append(pltpu.make_async_copy(laid.at[p], out_ref.at[p], out_sems.at[p]))
        stores[-1].start()
    for store in stores:
        store.wait()


def sum_terms(local_ref, term_ref, total, block):
    total[...] = jnp.zeros(total.shape, F32)

    def add(p, carry):
        for j in range(2):
            local = local_ref[2 * p + j]

            @pl.when(local >= 0)
            def _():
                rows = pl.ds(pl.multiple_of(local * block, block), block)
                total[rows, :] += term_ref[p, j * block : (j + 1) * block, :].astype(F32)

        return carry

    lax.fori_loop(0, term_ref.shape[0], add, 0)


def sum_kernel(block, local_ref, term_ref, out_ref, total):
    sum_terms(local_ref, term_ref, total, block)
    out_ref[...] = total[...].astype(BF16)


def owner_kernel(block, local_ref, term_ref, *refs):
    early, (weight_ref, up_ref, sum_ref, grad_ref, send_ref) = refs[: CHUNKS - 1], refs[CHUNKS - 1 : CHUNKS + 4]
    total, weight, up, last, grad, sems, send_sems = refs[CHUNKS + 4 :]
    loads = [
        pltpu.make_async_copy(weight_ref, weight, sems.at[0]),
        pltpu.make_async_copy(up_ref, up, sems.at[1]),
    ]
    for load in loads:
        load.start()
    total[...] = jnp.zeros(total.shape, F32)
    sum_terms(local_ref, term_ref, total, block)
    for load in loads:
        load.wait()
    for g in range(total.shape[0] // block):
        rows = slice(g * block, (g + 1) * block)
        last[rows, :] = total[rows, :].astype(BF16)
        summed = jnp.dot(
            jnp.concatenate([ref[rows, :] for ref in early] + [last[rows, :]], axis=1),
            weight[...],
            preferred_element_type=F32,
        )
        logistic = jax.nn.sigmoid(summed)
        slope = logistic * (1.0 + summed * (1.0 - logistic))
        grad[rows, :] = (up[rows, :].astype(F32) * slope).astype(BF16)
    width = send_ref.shape[2]
    stores = []
    for s in range(2 * send_ref.shape[0]):
        local = jnp.maximum(local_ref[s], 0)
        rows = pl.ds(pl.multiple_of(local * block, block), block)
        stores.append(
            pltpu.make_async_copy(
                grad.at[rows, pl.ds(0, width)],
                send_ref.at[s // 2, pl.ds(s % 2 * block, block)],
                send_sems.at[s],
            )
        )
    stores.append(pltpu.make_async_copy(last, sum_ref, sems.at[2]))
    stores.append(pltpu.make_async_copy(grad, grad_ref, sems.at[3]))
    run_all(stores)


def lay_out(local_ref, grad_ref, send_ref, chunk, block):
    width = send_ref.shape[2]
    cols = slice(chunk * width, (chunk + 1) * width)
    for p in range(send_ref.shape[0]):
        for j in range(2):
            local = jnp.maximum(local_ref[2 * p + j], 0)
            rows = pl.ds(pl.multiple_of(local * block, block), block)
            send_ref[p, j * block : (j + 1) * block, :] = grad_ref[rows, cols]


def finish_kernel(block, local_ref, *refs):
    parts, (grad_ref, weight_ref, out_ref), (*send_refs, dw_ref) = (
        refs[:CHUNKS],
        refs[CHUNKS : CHUNKS + 3],
        refs[CHUNKS + 3 :],
    )
    for k, send_ref in enumerate(send_refs):
        lay_out(local_ref, grad_ref, send_ref, k + 1, block)
    weight = weight_ref[...]
    dw = jnp.zeros(dw_ref.shape, F32)
    for g in range(out_ref.shape[0] // block):
        rows = slice(g * block, (g + 1) * block)
        aggregated = jnp.concatenate([ref[rows, :] for ref in parts], axis=1)
        summed = jnp.dot(aggregated, weight, preferred_element_type=F32)
        out_ref[rows, :] = (summed * jax.nn.sigmoid(summed)).astype(BF16)
        dw = dw + lax.dot_general(
            aggregated, grad_ref[rows, :], (((0,), (0,)), ((), ())), preferred_element_type=F32
        )
    dw_ref[...] = dw


def backward_kernel(block, *refs):
    lists, (near_tiles, far_tiles, near, far), outs = refs[:8], refs[8:12], refs[12:18]
    held, laid, sems = refs[18:]
    held[...] = jnp.zeros(held.shape, F32)
    for (count_ref, tile_ref, grad_ref, place_ref), tiles, grads in (
        (lists[:4], near_tiles, near),
        (lists[4:], far_tiles, far),
    ):

        def group(i, carry):
            entries = [i * GROUP + u for u in range(GROUP)]
            products = [
                jnp.dot(
                    tiles[tile_ref[e]],
                    grads[grad_ref[e] // 2, pl.ds(pl.multiple_of(grad_ref[e] % 2 * block, block), block), :],
                    preferred_element_type=F32,
                )
                for e in entries
            ]
            for e, product in zip(entries, products):
                held[pl.ds(pl.multiple_of(place_ref[e] * block, block), block), :] += product
            return carry

        lax.fori_loop(0, (count_ref[0] + GROUP - 1) // GROUP, group, 0)
    own, across, twice, across_twice, plus, minus = outs
    rows = own.shape[0]
    order = [
        own, plus.at[pl.ds(0, rows)], twice, minus.at[pl.ds(0, rows)],
        across, plus.at[pl.ds(rows, rows)], across_twice, minus.at[pl.ds(rows, rows)],
    ]
    stores = []
    for k, out in enumerate(order):
        laid[k] = held[k * rows : (k + 1) * rows, :].astype(BF16)
        stores.append(pltpu.make_async_copy(laid.at[k], out, sems.at[k]))
        stores[-1].start()
    for store in stores:
        store.wait()


def body(hidden, weight, adjacency, tile_target, tile_source, upstream, labels):
    block = adjacency.shape[1]
    slots = adjacency.shape[0]
    own_rows, width = hidden.shape
    own_blocks = own_rows // block
    row_count = lax.axis_size("rows")
    blk_count = lax.axis_size("blk")
    share = width // CHUNKS
    me = lax.axis_index("blk")
    columns = [slice(k * share, (k + 1) * share) for k in range(CHUNKS)]

    def move(value, dx, dy, dc):
        return lax.ppermute(value, "blk", blk_pairs(blk_count, dx, dy, dc))

    order = jnp.arange(slots, dtype=jnp.int32)
    peer = tile_target // own_blocks
    earlier = (peer[:, None] == peer[None, :]) & (order[None, :] < order[:, None])
    rank = jnp.sum(earlier.astype(jnp.int32), axis=1)
    spot = jnp.where(peer < row_count, peer * 2 + rank, -1)
    at = (spot[:, None] == order[None, :]).astype(jnp.int32)
    slot_at = jnp.sum(at * (order[:, None] + 1), axis=0) - 1
    local_at = jnp.sum(at * (tile_target[:, None] % own_blocks + 1), axis=0) - 1
    source_at = jnp.sum(at * (tile_source[:, None] + 1), axis=0) - 1
    holder = source_at // own_blocks
    dx = (holder // 4 - me // 4) % 4
    dy = (holder // 2 - me // 2) % 2
    dc = (holder - me) % 2
    inner = (dy * 4 + dx) * own_blocks + source_at % own_blocks
    places = 8 * own_blocks
    panel_at = jnp.where(source_at >= 0, dc * places + inner, -1)
    near_place = jnp.where((source_at >= 0) & (dc == 0), inner, places)
    cross_place = jnp.where((source_at >= 0) & (dc == 1), inner, places)

    def side_list(slot, place):
        used = (place < places).astype(jnp.int32)
        before = (order[None, :] < order[:, None]).astype(jnp.int32)
        used_before = jnp.sum(before * used[None, :], axis=1)
        count = jnp.sum(used).reshape(1)
        position = jnp.where(used > 0, used_before, count + order - used_before)
        chosen = (position[:, None] == order[None, :]).astype(jnp.int32)
        values = (jnp.maximum(slot, 0), order, place)
        return [count] + [jnp.sum(chosen * value[:, None], axis=0) for value in values]

    far = move(jnp.stack([slot_at, cross_place]), 0, 0, 1)
    lists = side_list(slot_at, near_place) + side_list(far[0], far[1])

    turned = jnp.swapaxes(adjacency, 1, 2)
    far_turned = move(turned, 0, 0, 1)
    marked = after(
        upstream * labels.astype(BF16)[:, None], turned, far_turned, *lists
    )

    def forward(shards, note):
        return pl.pallas_call(
            forward_kernel,
            out_shape=jax.ShapeDtypeStruct((row_count, 2 * block + note, share), BF16),
            in_specs=[SMEM_SPEC] * 3 + [ANY_SPEC] * (1 + len(shards)),
            out_specs=HBM_SPEC,
            scratch_shapes=[
                pltpu.VMEM((blk_count, own_rows, share), BF16),
                pltpu.VMEM(adjacency.shape, BF16),
                pltpu.VMEM((row_count, 2 * block + note, share), BF16),
                pltpu.SemaphoreType.DMA((blk_count + 1,)),
                pltpu.SemaphoreType.DMA((row_count,)),
            ],
            compiler_params=SMALL,
            cost_estimate=pl.CostEstimate(
                flops=2 * slots * block * block * share,
                bytes_accessed=2 * own_rows * blk_count * share,
                transcendentals=0,
            ),
        )(slot_at, panel_at, local_at, adjacency, *shards)

    def exchange(value):
        return lax.all_to_all(value, "rows", 0, 0, tiled=True)

    def spread(pair):
        return [move(pair, -1, 0, 0), move(pair, 1, 0, 0)]

    def both_cores(near, *others):
        held = near[:-1] + [after(near[-1], *others)]
        return near + [move(value, 0, 0, 1) for value in held]

    own = hidden[:, columns[0]]
    twice, across = move(own, 2, 0, 0), move(own, 0, 1, 0)
    pair = after(jnp.concatenate([own, across]), twice, slot_at, panel_at, local_at)
    pairs = spread(pair)
    near = [own, across, twice, move(twice, 0, 1, 0), *pairs]
    own = after(hidden[:, columns[1]], twice, across)
    across = move(own, 0, 1, 0)
    sums = forward(both_cores(near, across), NOTE)
    twice = move(after(own, *pairs), 2, 0, 0)
    got = [exchange(sums)]
    pairs = spread(after(jnp.concatenate([own, across]), sums, twice))
    near = [own, across, twice, move(twice, 0, 1, 0), *pairs]
    got.append(exchange(forward(both_cores(near), 0)))
    local_got = got[0][:, 2 * block : 2 * block + 2, 0].astype(jnp.int32).reshape(-1)

    early = [
        pl.pallas_call(
            lambda *refs: sum_kernel(block, *refs),
            out_shape=jax.ShapeDtypeStruct((own_rows, share), BF16),
            in_specs=[SMEM_SPEC, VMEM_SPEC],
            out_specs=VMEM_SPEC,
            scratch_shapes=[pltpu.VMEM((own_rows, share), F32)],
            compiler_params=SMALL,
            cost_estimate=pl.CostEstimate(
                flops=slots * block * share, bytes_accessed=2 * slots * block * share, transcendentals=0
            ),
        )(local_got, term)
        for term in got[:-1]
    ]
    last_sums, grad, send = pl.pallas_call(
        lambda *refs: owner_kernel(block, *refs),
        out_shape=(
            jax.ShapeDtypeStruct((own_rows, share), BF16),
            jax.ShapeDtypeStruct((own_rows, width), BF16),
            jax.ShapeDtypeStruct((row_count, 2 * block, share), BF16),
        ),
        in_specs=[SMEM_SPEC] + [VMEM_SPEC] * CHUNKS + [ANY_SPEC] * 2,
        out_specs=(HBM_SPEC,) * 3,
        scratch_shapes=[
            pltpu.VMEM((own_rows, share), F32),
            pltpu.VMEM((width, width), BF16),
            pltpu.VMEM((own_rows, width), BF16),
            pltpu.VMEM((own_rows, share), BF16),
            pltpu.VMEM((own_rows, width), BF16),
            pltpu.SemaphoreType.DMA((4,)),
            pltpu.SemaphoreType.DMA((slots,)),
        ],
        compiler_params=LARGE,
        cost_estimate=pl.CostEstimate(
            flops=2 * own_rows * width * width,
            bytes_accessed=10 * own_rows * width,
            transcendentals=own_rows * width,
        ),
    )(local_got, got[-1], *early, weight, marked)
    back = [exchange(send)]
    tail_rows = width // blk_count * CHUNKS
    output, *sends, local_grad = pl.pallas_call(
        lambda *refs: finish_kernel(block, *refs),
        out_shape=(
            jax.ShapeDtypeStruct((own_rows, width), BF16),
            *[
                jax.ShapeDtypeStruct((row_count, 2 * block + tail, share), BF16)
                for tail in [0] * (CHUNKS - 2) + [tail_rows]
            ],
            jax.ShapeDtypeStruct((width, width), F32),
        ),
        in_specs=[SMEM_SPEC] + [VMEM_SPEC] * (CHUNKS + 2),
        out_specs=(VMEM_SPEC,) * (CHUNKS + 1),
        compiler_params=LARGE,
        cost_estimate=pl.CostEstimate(
            flops=4 * own_rows * width * width,
            bytes_accessed=8 * own_rows * width,
            transcendentals=own_rows * width,
        ),
    )(local_got, *early, last_sums, grad, weight)

    def backward(near):
        far_near = move(near[:, : 2 * block, :], 0, 0, 1)
        return pl.pallas_call(
            lambda *refs: backward_kernel(block, *refs),
            out_shape=[
                jax.ShapeDtypeStruct((count * own_rows, share), BF16) for count in (1, 1, 1, 1, 2, 2)
            ],
            in_specs=[SMEM_SPEC] * 8 + [VMEM_SPEC] * 4,
            out_specs=[HBM_SPEC] * 6,
            scratch_shapes=[
                pltpu.VMEM(((places + 1) * block, share), F32),
                pltpu.VMEM((8, own_rows, share), BF16),
                pltpu.SemaphoreType.DMA((8,)),
            ],
            compiler_params=MIDDLE,
            cost_estimate=pl.CostEstimate(
                flops=2 * slots * block * block * share,
                bytes_accessed=2 * own_rows * blk_count * share,
                transcendentals=0,
            ),
        )(*lists, turned, far_turned, near, far_near)

    def wide_sum(*values):
        return sum(value.astype(F32) for value in values).astype(BF16)

    def first_sums(parts):
        own, across, twice, across_twice, plus, minus = parts
        from_minus, from_plus = move(plus, 1, 0, 0), move(minus, -1, 0, 0)
        twice = wide_sum(twice, move(across_twice, 0, 1, 0))
        own = wide_sum(own, from_minus[:own_rows], from_plus[:own_rows])
        across = wide_sum(across, from_minus[own_rows:], from_plus[own_rows:])
        return [own, across, twice]

    def last_moves(parts):
        own, across, twice = parts
        return [own, move(across, 0, 1, 0), move(twice, 2, 0, 0)]

    x, y, c = me // 4, (me // 2) % 2, me % 2

    def halve(value, bit, dy, dc):
        half = value.shape[0] // 2
        keep = lax.dynamic_slice_in_dim(value, bit * half, half)
        return keep + move(lax.dynamic_slice_in_dim(value, (1 - bit) * half, half), 0, dy, dc)

    value = halve(halve(local_grad, c, 0, 1), y, 1, 0)
    rows = value.shape[0] // 4
    terms = [lax.dynamic_slice_in_dim(value, ((x + step) % 4) * rows, rows) for step in range(4)]
    piece = terms[0] + sum(move(terms[step], step, 0, 0) for step in (1, 2, 3))
    piece = jnp.concatenate([piece[:, cols] for cols in columns]).astype(BF16)
    sends[-1] = sends[-1].at[:, 2 * block :, :].set(piece[None])

    back.append(exchange(after(sends[-1], back[0])))
    piece = jnp.sum(back[-1][:, 2 * block :, :].astype(F32), axis=0)
    half_way = first_sums(backward(back[0]))
    last = backward(after(back[1], *half_way))
    received = last_moves(half_way)
    last_half_way = first_sums(after(tuple(last), *received))
    d_proj = [wide_sum(*received), wide_sum(*last_moves(last_half_way))]
    d_hidden = sum(
        lax.dot_general(
            part, weight[:, cols], (((1,), (1,)), ((), ())), preferred_element_type=F32
        )
        for part, cols in zip(d_proj, columns)
    ).astype(BF16)

    pieces = lax.all_to_all(
        jnp.broadcast_to(piece[None], (blk_count, *piece.shape)), "blk", 0, 0, tiled=True
    )
    pieces = pieces.reshape(4, 2, 2, CHUNKS, rows, share).transpose(2, 1, 0, 4, 3, 5)
    node_total = own_rows * row_count * blk_count
    d_weight = pieces.reshape(width, width) * (1.0 / math.sqrt(node_total))
    return (output, d_hidden, d_weight)


def solution(mesh):
    both = ("rows", "blk")
    return jax.shard_map(
        body,
        mesh=mesh,
        in_specs=(P(both, None), P(), P(both, None, None), P(both), P(both), P(both, None), P(both)),
        out_specs=(P(both, None), P(both, None), P()),
        check_vma=False,
    )
```

```python
import math

import jax
import jax.numpy as jnp
from jax import lax
from jax.experimental import pallas as pl
from jax.experimental.pallas import tpu as pltpu
from jax.sharding import PartitionSpec as P

BF16 = jnp.bfloat16
F32 = jnp.float32
CHUNKS = 2
NOTE = 16
GROUP = 4
SMEM_SPEC = pl.BlockSpec(memory_space=pltpu.SMEM)
VMEM_SPEC = pl.BlockSpec(memory_space=pltpu.VMEM)
ANY_SPEC = pl.BlockSpec(memory_space=pl.ANY)
HBM_SPEC = pl.BlockSpec(memory_space=pltpu.HBM)
MIB = 1024 * 1024
SMALL = pltpu.CompilerParams(vmem_limit_bytes=20 * MIB)
MIDDLE = pltpu.CompilerParams(vmem_limit_bytes=44 * MIB)
LARGE = pltpu.CompilerParams(vmem_limit_bytes=56 * MIB)


def after(value, *others):
    return lax.optimization_barrier((value, *others))[0]


def blk_pairs(blk_count, dx, dy, dc):
    x_count = blk_count // 4
    pairs = []
    for b in range(blk_count):
        x, y, c = b // 4, (b // 2) % 2, b % 2
        pairs.append((b, ((x + dx) % x_count) * 4 + ((y + dy) % 2) * 2 + (c + dc) % 2))
    return pairs


def run_all(copies):
    for copy in copies:
        copy.start()
    for copy in copies:
        copy.wait()


def forward_kernel(slot_ref, source_ref, local_ref, tiles_ref, *refs):
    shards, out_ref, (held, tiles, laid, sems, out_sems) = refs[:-6], refs[-6], refs[-5:]
    rows = held.shape[1]
    copies = [pltpu.make_async_copy(tiles_ref, tiles, sems.at[0])]
    side = len(shards) // 2
    for core in range(2):
        own, across, twice, across_twice, plus, minus = shards[core * side : (core + 1) * side]
        parts = [
            own, plus.at[pl.ds(0, rows)], twice, minus.at[pl.ds(0, rows)],
            across, plus.at[pl.ds(rows, rows)],
            across_twice, minus.at[pl.ds(rows, rows)],
        ]
        for part in parts:
            place = len(copies) - 1
            copies.append(pltpu.make_async_copy(part, held.at[place], sems.at[place + 1]))
    run_all(copies)
    block = tiles.shape[1]
    noted = out_ref.shape[1] > 2 * block
    row = lax.broadcasted_iota(jnp.int32, (NOTE, out_ref.shape[2]), 0)
    stores = []
    for p in range(out_ref.shape[0]):
        for j in range(2):
            slot = jnp.maximum(slot_ref[2 * p + j], 0)
            source = jnp.maximum(source_ref[2 * p + j], 0)
            panel = held[source // 8, pl.ds(pl.multiple_of((source % 8) * block, block), block), :]
            product = jnp.dot(tiles[slot], panel, preferred_element_type=F32)
            laid[p, j * block : (j + 1) * block, :] = product.astype(BF16)
        if noted:
            note = jnp.where(row == 0, local_ref[2 * p], local_ref[2 * p + 1])
            laid[p, 2 * block :, :] = note.astype(F32).astype(BF16)
        stores.append(pltpu.make_async_copy(laid.at[p], out_ref.at[p], out_sems.at[p]))
        stores[-1].start()
    for store in stores:
        store.wait()


def sum_terms(local_ref, term_ref, total, block):
    total[...] = jnp.zeros(total.shape, F32)

    def add(p, carry):
        for j in range(2):
            local = local_ref[2 * p + j]

            @pl.when(local >= 0)
            def _():
                rows = pl.ds(pl.multiple_of(local * block, block), block)
                total[rows, :] += term_ref[p, j * block : (j + 1) * block, :].astype(F32)

        return carry

    lax.fori_loop(0, term_ref.shape[0], add, 0)


def sum_kernel(block, local_ref, term_ref, out_ref, total):
    sum_terms(local_ref, term_ref, total, block)
    out_ref[...] = total[...].astype(BF16)


def owner_kernel(block, local_ref, term_ref, *refs):
    early, (weight_ref, up_ref, sum_ref, grad_ref, send_ref) = refs[: CHUNKS - 1], refs[CHUNKS - 1 : CHUNKS + 4]
    total, weight, up, last, grad, sems, send_sems = refs[CHUNKS + 4 :]
    loads = [
        pltpu.make_async_copy(weight_ref, weight, sems.at[0]),
        pltpu.make_async_copy(up_ref, up, sems.at[1]),
    ]
    for load in loads:
        load.start()
    total[...] = jnp.zeros(total.shape, F32)
    sum_terms(local_ref, term_ref, total, block)
    for load in loads:
        load.wait()
    for g in range(total.shape[0] // block):
        rows = slice(g * block, (g + 1) * block)
        last[rows, :] = total[rows, :].astype(BF16)
        summed = jnp.dot(
            jnp.concatenate([ref[rows, :] for ref in early] + [last[rows, :]], axis=1),
            weight[...],
            preferred_element_type=F32,
        )
        logistic = jax.nn.sigmoid(summed)
        slope = logistic * (1.0 + summed * (1.0 - logistic))
        grad[rows, :] = (up[rows, :].astype(F32) * slope).astype(BF16)
    width = send_ref.shape[2]
    stores = []
    for s in range(2 * send_ref.shape[0]):
        local = jnp.maximum(local_ref[s], 0)
        rows = pl.ds(pl.multiple_of(local * block, block), block)
        stores.append(
            pltpu.make_async_copy(
                grad.at[rows, pl.ds(0, width)],
                send_ref.at[s // 2, pl.ds(s % 2 * block, block)],
                send_sems.at[s],
            )
        )
    stores.append(pltpu.make_async_copy(last, sum_ref, sems.at[2]))
    stores.append(pltpu.make_async_copy(grad, grad_ref, sems.at[3]))
    run_all(stores)


def lay_out(local_ref, grad_ref, send_ref, chunk, block):
    width = send_ref.shape[2]
    cols = slice(chunk * width, (chunk + 1) * width)
    for p in range(send_ref.shape[0]):
        for j in range(2):
            local = jnp.maximum(local_ref[2 * p + j], 0)
            rows = pl.ds(pl.multiple_of(local * block, block), block)
            send_ref[p, j * block : (j + 1) * block, :] = grad_ref[rows, cols]


def finish_kernel(block, local_ref, *refs):
    parts, (grad_ref, weight_ref, out_ref), (*send_refs, dw_ref) = (
        refs[:CHUNKS],
        refs[CHUNKS : CHUNKS + 3],
        refs[CHUNKS + 3 :],
    )
    for k, send_ref in enumerate(send_refs):
        lay_out(local_ref, grad_ref, send_ref, k + 1, block)
    weight = weight_ref[...]
    dw = jnp.zeros(dw_ref.shape, F32)
    for g in range(out_ref.shape[0] // block):
        rows = slice(g * block, (g + 1) * block)
        aggregated = jnp.concatenate([ref[rows, :] for ref in parts], axis=1)
        summed = jnp.dot(aggregated, weight, preferred_element_type=F32)
        out_ref[rows, :] = (summed * jax.nn.sigmoid(summed)).astype(BF16)
        dw = dw + lax.dot_general(
            aggregated, grad_ref[rows, :], (((0,), (0,)), ((), ())), preferred_element_type=F32
        )
    dw_ref[...] = dw


def backward_kernel(block, *refs):
    lists, (near_tiles, far_tiles, near, far), outs = refs[:8], refs[8:12], refs[12:18]
    held, laid, sems = refs[18:]
    held[...] = jnp.zeros(held.shape, F32)
    for (count_ref, tile_ref, grad_ref, place_ref), tiles, grads in (
        (lists[:4], near_tiles, near),
        (lists[4:], far_tiles, far),
    ):

        def group(i, carry):
            entries = [i * GROUP + u for u in range(GROUP)]
            products = [
                jnp.dot(
                    tiles[tile_ref[e]],
                    grads[grad_ref[e] // 2, pl.ds(pl.multiple_of(grad_ref[e] % 2 * block, block), block), :],
                    preferred_element_type=F32,
                )
                for e in entries
            ]
            for e, product in zip(entries, products):
                held[pl.ds(pl.multiple_of(place_ref[e] * block, block), block), :] += product
            return carry

        lax.fori_loop(0, (count_ref[0] + GROUP - 1) // GROUP, group, 0)
    own, across, twice, across_twice, plus, minus = outs
    rows = own.shape[0]
    order = [
        own, plus.at[pl.ds(0, rows)], twice, minus.at[pl.ds(0, rows)],
        across, plus.at[pl.ds(rows, rows)], across_twice, minus.at[pl.ds(rows, rows)],
    ]
    stores = []
    for k, out in enumerate(order):
        laid[k] = held[k * rows : (k + 1) * rows, :].astype(BF16)
        stores.append(pltpu.make_async_copy(laid.at[k], out, sems.at[k]))
        stores[-1].start()
    for store in stores:
        store.wait()


def body(hidden, weight, adjacency, tile_target, tile_source, upstream, labels):
    block = adjacency.shape[1]
    slots = adjacency.shape[0]
    own_rows, width = hidden.shape
    own_blocks = own_rows // block
    row_count = lax.axis_size("rows")
    blk_count = lax.axis_size("blk")
    share = width // CHUNKS
    me = lax.axis_index("blk")
    columns = [slice(k * share, (k + 1) * share) for k in range(CHUNKS)]

    def move(value, dx, dy, dc):
        return lax.ppermute(value, "blk", blk_pairs(blk_count, dx, dy, dc))

    order = jnp.arange(slots, dtype=jnp.int32)
    peer = tile_target // own_blocks
    earlier = (peer[:, None] == peer[None, :]) & (order[None, :] < order[:, None])
    rank = jnp.sum(earlier.astype(jnp.int32), axis=1)
    spot = jnp.where(peer < row_count, peer * 2 + rank, -1)
    at = (spot[:, None] == order[None, :]).astype(jnp.int32)
    slot_at = jnp.sum(at * (order[:, None] + 1), axis=0) - 1
    local_at = jnp.sum(at * (tile_target[:, None] % own_blocks + 1), axis=0) - 1
    source_at = jnp.sum(at * (tile_source[:, None] + 1), axis=0) - 1
    holder = source_at // own_blocks
    dx = (holder // 4 - me // 4) % 4
    dy = (holder // 2 - me // 2) % 2
    dc = (holder - me) % 2
    inner = (dy * 4 + dx) * own_blocks + source_at % own_blocks
    places = 8 * own_blocks
    panel_at = jnp.where(source_at >= 0, dc * places + inner, -1)
    near_place = jnp.where((source_at >= 0) & (dc == 0), inner, places)
    cross_place = jnp.where((source_at >= 0) & (dc == 1), inner, places)

    def side_list(slot, place):
        used = (place < places).astype(jnp.int32)
        before = (order[None, :] < order[:, None]).astype(jnp.int32)
        used_before = jnp.sum(before * used[None, :], axis=1)
        count = jnp.sum(used).reshape(1)
        position = jnp.where(used > 0, used_before, count + order - used_before)
        chosen = (position[:, None] == order[None, :]).astype(jnp.int32)
        values = (jnp.maximum(slot, 0), order, place)
        return [count] + [jnp.sum(chosen * value[:, None], axis=0) for value in values]

    far = move(jnp.stack([slot_at, cross_place]), 0, 0, 1)
    lists = side_list(slot_at, near_place) + side_list(far[0], far[1])

    turned = jnp.swapaxes(adjacency, 1, 2)
    far_turned = move(turned, 0, 0, 1)
    marked = after(
        upstream * labels.astype(BF16)[:, None], turned, far_turned, *lists
    )

    def forward(shards, note):
        return pl.pallas_call(
            forward_kernel,
            out_shape=jax.ShapeDtypeStruct((row_count, 2 * block + note, share), BF16),
            in_specs=[SMEM_SPEC] * 3 + [ANY_SPEC] * (1 + len(shards)),
            out_specs=HBM_SPEC,
            scratch_shapes=[
                pltpu.VMEM((blk_count, own_rows, share), BF16),
                pltpu.VMEM(adjacency.shape, BF16),
                pltpu.VMEM((row_count, 2 * block + note, share), BF16),
                pltpu.SemaphoreType.DMA((blk_count + 1,)),
                pltpu.SemaphoreType.DMA((row_count,)),
            ],
            compiler_params=SMALL,
            cost_estimate=pl.CostEstimate(
                flops=2 * slots * block * block * share,
                bytes_accessed=2 * own_rows * blk_count * share,
                transcendentals=0,
            ),
        )(slot_at, panel_at, local_at, adjacency, *shards)

    def exchange(value):
        return lax.all_to_all(value, "rows", 0, 0, tiled=True)

    def spread(pair):
        return [move(pair, -1, 0, 0), move(pair, 1, 0, 0)]

    def both_cores(near, *others):
        held = near[:-1] + [after(near[-1], *others)]
        return near + [move(value, 0, 0, 1) for value in held]

    own = hidden[:, columns[0]]
    twice, across = move(own, 2, 0, 0), move(own, 0, 1, 0)
    pair = after(jnp.concatenate([own, across]), twice, slot_at, panel_at, local_at)
    pairs = spread(pair)
    near = [own, across, twice, move(twice, 0, 1, 0), *pairs]
    own = after(hidden[:, columns[1]], twice, across)
    across = move(own, 0, 1, 0)
    sums = forward(both_cores(near, across), NOTE)
    twice = move(after(own, *pairs), 2, 0, 0)
    got = [exchange(sums)]
    pairs = spread(after(jnp.concatenate([own, across]), sums, twice))
    near = [own, across, twice, move(twice, 0, 1, 0), *pairs]
    got.append(exchange(forward(both_cores(near), 0)))
    local_got = got[0][:, 2 * block : 2 * block + 2, 0].astype(jnp.int32).reshape(-1)

    early = [
        pl.pallas_call(
            lambda *refs: sum_kernel(block, *refs),
            out_shape=jax.ShapeDtypeStruct((own_rows, share), BF16),
            in_specs=[SMEM_SPEC, VMEM_SPEC],
            out_specs=VMEM_SPEC,
            scratch_shapes=[pltpu.VMEM((own_rows, share), F32)],
            compiler_params=SMALL,
            cost_estimate=pl.CostEstimate(
                flops=slots * block * share, bytes_accessed=2 * slots * block * share, transcendentals=0
            ),
        )(local_got, term)
        for term in got[:-1]
    ]
    last_sums, grad, send = pl.pallas_call(
        lambda *refs: owner_kernel(block, *refs),
        out_shape=(
            jax.ShapeDtypeStruct((own_rows, share), BF16),
            jax.ShapeDtypeStruct((own_rows, width), BF16),
            jax.ShapeDtypeStruct((row_count, 2 * block, share), BF16),
        ),
        in_specs=[SMEM_SPEC] + [VMEM_SPEC] * CHUNKS + [ANY_SPEC] * 2,
        out_specs=(HBM_SPEC,) * 3,
        scratch_shapes=[
            pltpu.VMEM((own_rows, share), F32),
            pltpu.VMEM((width, width), BF16),
            pltpu.VMEM((own_rows, width), BF16),
            pltpu.VMEM((own_rows, share), BF16),
            pltpu.VMEM((own_rows, width), BF16),
            pltpu.SemaphoreType.DMA((4,)),
            pltpu.SemaphoreType.DMA((slots,)),
        ],
        compiler_params=LARGE,
        cost_estimate=pl.CostEstimate(
            flops=2 * own_rows * width * width,
            bytes_accessed=10 * own_rows * width,
            transcendentals=own_rows * width,
        ),
    )(local_got, got[-1], *early, weight, marked)
    back = [exchange(send)]
    tail_rows = width // blk_count * CHUNKS
    output, *sends, local_grad = pl.pallas_call(
        lambda *refs: finish_kernel(block, *refs),
        out_shape=(
            jax.ShapeDtypeStruct((own_rows, width), BF16),
            *[
                jax.ShapeDtypeStruct((row_count, 2 * block + tail, share), BF16)
                for tail in [0] * (CHUNKS - 2) + [tail_rows]
            ],
            jax.ShapeDtypeStruct((width, width), F32),
        ),
        in_specs=[SMEM_SPEC] + [VMEM_SPEC] * (CHUNKS + 2),
        out_specs=(VMEM_SPEC,) * (CHUNKS + 1),
        compiler_params=LARGE,
        cost_estimate=pl.CostEstimate(
            flops=4 * own_rows * width * width,
            bytes_accessed=8 * own_rows * width,
            transcendentals=own_rows * width,
        ),
    )(local_got, *early, last_sums, grad, weight)

    def backward(near):
        far_near = move(near[:, : 2 * block, :], 0, 0, 1)
        return pl.pallas_call(
            lambda *refs: backward_kernel(block, *refs),
            out_shape=[
                jax.ShapeDtypeStruct((count * own_rows, share), BF16) for count in (1, 1, 1, 1, 2, 2)
            ],
            in_specs=[SMEM_SPEC] * 8 + [VMEM_SPEC] * 4,
            out_specs=[HBM_SPEC] * 6,
            scratch_shapes=[
                pltpu.VMEM(((places + 1) * block, share), F32),
                pltpu.VMEM((8, own_rows, share), BF16),
                pltpu.SemaphoreType.DMA((8,)),
            ],
            compiler_params=MIDDLE,
            cost_estimate=pl.CostEstimate(
                flops=2 * slots * block * block * share,
                bytes_accessed=2 * own_rows * blk_count * share,
                transcendentals=0,
            ),
        )(*lists, turned, far_turned, near, far_near)

    def wide_sum(*values):
        return sum(value.astype(F32) for value in values).astype(BF16)

    def first_sums(parts):
        own, across, twice, across_twice, plus, minus = parts
        from_minus, from_plus = move(plus, 1, 0, 0), move(minus, -1, 0, 0)
        twice = after(wide_sum(twice, move(across_twice, 0, 1, 0)), from_minus, from_plus)
        own = wide_sum(own, from_minus[:own_rows], from_plus[:own_rows])
        across = wide_sum(across, from_minus[own_rows:], from_plus[own_rows:])
        return [own, across, twice]

    def last_moves(parts):
        own, across, twice = parts
        return [own, move(across, 0, 1, 0), move(twice, 2, 0, 0)]

    x, y, c = me // 4, (me // 2) % 2, me % 2

    def halve(value, bit, dy, dc):
        half = value.shape[0] // 2
        keep = lax.dynamic_slice_in_dim(value, bit * half, half)
        return keep + move(lax.dynamic_slice_in_dim(value, (1 - bit) * half, half), 0, dy, dc)

    value = halve(halve(local_grad, c, 0, 1), y, 1, 0)
    rows = value.shape[0] // 4
    terms = [lax.dynamic_slice_in_dim(value, ((x + step) % 4) * rows, rows) for step in range(4)]
    piece = terms[0] + sum(move(terms[step], step, 0, 0) for step in (1, 2, 3))
    piece = jnp.concatenate([piece[:, cols] for cols in columns]).astype(BF16)
    sends[-1] = sends[-1].at[:, 2 * block :, :].set(piece[None])

    back.append(exchange(after(sends[-1], back[0])))
    piece = jnp.sum(back[-1][:, 2 * block :, :].astype(F32), axis=0)
    half_way = first_sums(backward(back[0]))
    last = backward(after(back[1], *half_way))
    received = last_moves(half_way)
    last_half_way = first_sums(after(tuple(last), *received))
    d_proj = [wide_sum(*received), wide_sum(*last_moves(last_half_way))]
    d_hidden = sum(
        lax.dot_general(
            part, weight[:, cols], (((1,), (1,)), ((), ())), preferred_element_type=F32
        )
        for part, cols in zip(d_proj, columns)
    ).astype(BF16)

    pieces = lax.all_to_all(
        jnp.broadcast_to(piece[None], (blk_count, *piece.shape)), "blk", 0, 0, tiled=True
    )
    pieces = pieces.reshape(4, 2, 2, CHUNKS, rows, share).transpose(2, 1, 0, 4, 3, 5)
    node_total = own_rows * row_count * blk_count
    d_weight = pieces.reshape(width, width) * (1.0 / math.sqrt(node_total))
    return (output, d_hidden, d_weight)


def solution(mesh):
    both = ("rows", "blk")
    return jax.shard_map(
        body,
        mesh=mesh,
        in_specs=(P(both, None), P(), P(both, None, None), P(both), P(both), P(both, None), P(both)),
        out_specs=(P(both, None), P(both, None), P()),
        check_vma=False,
    )
```

```python
import math

import jax
import jax.numpy as jnp
from jax import lax
from jax.experimental import pallas as pl
from jax.experimental.pallas import tpu as pltpu
from jax.sharding import PartitionSpec as P

BF16 = jnp.bfloat16
F32 = jnp.float32
CHUNKS = 2
NOTE = 16
GROUP = 4
SMEM_SPEC = pl.BlockSpec(memory_space=pltpu.SMEM)
VMEM_SPEC = pl.BlockSpec(memory_space=pltpu.VMEM)
ANY_SPEC = pl.BlockSpec(memory_space=pl.ANY)
HBM_SPEC = pl.BlockSpec(memory_space=pltpu.HBM)
MIB = 1024 * 1024
SMALL = pltpu.CompilerParams(vmem_limit_bytes=20 * MIB)
MIDDLE = pltpu.CompilerParams(vmem_limit_bytes=50 * MIB)
LARGE = pltpu.CompilerParams(vmem_limit_bytes=56 * MIB)


def after(value, *others):
    return lax.optimization_barrier((value, *others))[0]


def blk_pairs(blk_count, dx, dy, dc):
    x_count = blk_count // 4
    pairs = []
    for b in range(blk_count):
        x, y, c = b // 4, (b // 2) % 2, b % 2
        pairs.append((b, ((x + dx) % x_count) * 4 + ((y + dy) % 2) * 2 + (c + dc) % 2))
    return pairs


def run_all(copies):
    for copy in copies:
        copy.start()
    for copy in copies:
        copy.wait()


def forward_kernel(slot_ref, source_ref, local_ref, tiles_ref, *refs):
    shards, out_ref, (held, tiles, laid, sems, out_sems) = refs[:-6], refs[-6], refs[-5:]
    rows = held.shape[1]
    copies = [pltpu.make_async_copy(tiles_ref, tiles, sems.at[0])]
    side = len(shards) // 2
    for core in range(2):
        own, across, twice, across_twice, plus, minus = shards[core * side : (core + 1) * side]
        parts = [
            own, plus.at[pl.ds(0, rows)], twice, minus.at[pl.ds(0, rows)],
            across, plus.at[pl.ds(rows, rows)],
            across_twice, minus.at[pl.ds(rows, rows)],
        ]
        for part in parts:
            place = len(copies) - 1
            copies.append(pltpu.make_async_copy(part, held.at[place], sems.at[place + 1]))
    run_all(copies)
    block = tiles.shape[1]
    noted = out_ref.shape[1] > 2 * block
    row = lax.broadcasted_iota(jnp.int32, (NOTE, out_ref.shape[2]), 0)
    stores = []
    for p in range(out_ref.shape[0]):
        for j in range(2):
            slot = jnp.maximum(slot_ref[2 * p + j], 0)
            source = jnp.maximum(source_ref[2 * p + j], 0)
            panel = held[source // 8, pl.ds(pl.multiple_of((source % 8) * block, block), block), :]
            product = jnp.dot(tiles[slot], panel, preferred_element_type=F32)
            laid[p, j * block : (j + 1) * block, :] = product.astype(BF16)
        if noted:
            note = jnp.where(row == 0, local_ref[2 * p], local_ref[2 * p + 1])
            laid[p, 2 * block :, :] = note.astype(F32).astype(BF16)
        stores.append(pltpu.make_async_copy(laid.at[p], out_ref.at[p], out_sems.at[p]))
        stores[-1].start()
    for store in stores:
        store.wait()


def sum_terms(local_ref, term_ref, total, block):
    total[...] = jnp.zeros(total.shape, F32)

    def add(p, carry):
        for j in range(2):
            local = local_ref[2 * p + j]

            @pl.when(local >= 0)
            def _():
                rows = pl.ds(pl.multiple_of(local * block, block), block)
                total[rows, :] += term_ref[p, j * block : (j + 1) * block, :].astype(F32)

        return carry

    lax.fori_loop(0, term_ref.shape[0], add, 0)


def sum_kernel(block, local_ref, term_ref, out_ref, total):
    sum_terms(local_ref, term_ref, total, block)
    out_ref[...] = total[...].astype(BF16)


def owner_kernel(block, local_ref, term_ref, *refs):
    early, (weight_ref, up_ref, sum_ref, grad_ref, send_ref) = refs[: CHUNKS - 1], refs[CHUNKS - 1 : CHUNKS + 4]
    total, weight, up, last, grad, sems, send_sems = refs[CHUNKS + 4 :]
    loads = [
        pltpu.make_async_copy(weight_ref, weight, sems.at[0]),
        pltpu.make_async_copy(up_ref, up, sems.at[1]),
    ]
    for load in loads:
        load.start()
    total[...] = jnp.zeros(total.shape, F32)
    sum_terms(local_ref, term_ref, total, block)
    for load in loads:
        load.wait()
    for g in range(total.shape[0] // block):
        rows = slice(g * block, (g + 1) * block)
        last[rows, :] = total[rows, :].astype(BF16)
        summed = jnp.dot(
            jnp.concatenate([ref[rows, :] for ref in early] + [last[rows, :]], axis=1),
            weight[...],
            preferred_element_type=F32,
        )
        logistic = jax.nn.sigmoid(summed)
        slope = logistic * (1.0 + summed * (1.0 - logistic))
        grad[rows, :] = (up[rows, :].astype(F32) * slope).astype(BF16)
    width = send_ref.shape[2]
    stores = []
    for s in range(2 * send_ref.shape[0]):
        local = jnp.maximum(local_ref[s], 0)
        rows = pl.ds(pl.multiple_of(local * block, block), block)
        stores.append(
            pltpu.make_async_copy(
                grad.at[rows, pl.ds(0, width)],
                send_ref.at[s // 2, pl.ds(s % 2 * block, block)],
                send_sems.at[s],
            )
        )
    stores.append(pltpu.make_async_copy(last, sum_ref, sems.at[2]))
    stores.append(pltpu.make_async_copy(grad, grad_ref, sems.at[3]))
    run_all(stores)


def lay_out(local_ref, grad_ref, send_ref, chunk, block):
    width = send_ref.shape[2]
    cols = slice(chunk * width, (chunk + 1) * width)
    for p in range(send_ref.shape[0]):
        for j in range(2):
            local = jnp.maximum(local_ref[2 * p + j], 0)
            rows = pl.ds(pl.multiple_of(local * block, block), block)
            send_ref[p, j * block : (j + 1) * block, :] = grad_ref[rows, cols]


def finish_kernel(block, local_ref, *refs):
    parts, (grad_ref, weight_ref, out_ref), (*send_refs, dw_ref) = (
        refs[:CHUNKS],
        refs[CHUNKS : CHUNKS + 3],
        refs[CHUNKS + 3 :],
    )
    for k, send_ref in enumerate(send_refs):
        lay_out(local_ref, grad_ref, send_ref, k + 1, block)
    weight = weight_ref[...]
    dw = jnp.zeros(dw_ref.shape, F32)
    for g in range(out_ref.shape[0] // block):
        rows = slice(g * block, (g + 1) * block)
        aggregated = jnp.concatenate([ref[rows, :] for ref in parts], axis=1)
        summed = jnp.dot(aggregated, weight, preferred_element_type=F32)
        out_ref[rows, :] = (summed * jax.nn.sigmoid(summed)).astype(BF16)
        dw = dw + lax.dot_general(
            aggregated, grad_ref[rows, :], (((0,), (0,)), ((), ())), preferred_element_type=F32
        )
    dw_ref[...] = dw


def backward_kernel(block, *refs):
    lists, (near_tiles, far_tiles, near, far), outs = refs[:8], refs[8:12], refs[12:18]
    held, laid, sems = refs[18:]
    held[...] = jnp.zeros(held.shape, F32)
    for (count_ref, tile_ref, grad_ref, place_ref), tiles, grads in (
        (lists[:4], near_tiles, near),
        (lists[4:], far_tiles, far),
    ):

        def group(i, carry):
            entries = [i * GROUP + u for u in range(GROUP)]
            products = [
                jnp.dot(
                    tiles[tile_ref[e]],
                    grads[grad_ref[e] // 2, pl.ds(pl.multiple_of(grad_ref[e] % 2 * block, block), block), :],
                    preferred_element_type=F32,
                )
                for e in entries
            ]
            for e, product in zip(entries, products):
                held[pl.ds(pl.multiple_of(place_ref[e] * block, block), block), :] += product
            return carry

        lax.fori_loop(0, (count_ref[0] + GROUP - 1) // GROUP, group, 0)
    own, across, twice, across_twice, plus, minus = outs
    rows = own.shape[0]
    order = [
        own, plus.at[pl.ds(0, rows)], twice, minus.at[pl.ds(0, rows)],
        across, plus.at[pl.ds(rows, rows)], across_twice, minus.at[pl.ds(rows, rows)],
    ]
    stores = []
    for k, out in enumerate(order):
        laid[k] = held[k * rows : (k + 1) * rows, :].astype(BF16)
        stores.append(pltpu.make_async_copy(laid.at[k], out, sems.at[k]))
        stores[-1].start()
    for store in stores:
        store.wait()


def body(hidden, weight, adjacency, tile_target, tile_source, upstream, labels):
    block = adjacency.shape[1]
    slots = adjacency.shape[0]
    own_rows, width = hidden.shape
    own_blocks = own_rows // block
    row_count = lax.axis_size("rows")
    blk_count = lax.axis_size("blk")
    share = width // CHUNKS
    me = lax.axis_index("blk")
    columns = [slice(k * share, (k + 1) * share) for k in range(CHUNKS)]

    def move(value, dx, dy, dc):
        return lax.ppermute(value, "blk", blk_pairs(blk_count, dx, dy, dc))

    order = jnp.arange(slots, dtype=jnp.int32)
    peer = tile_target // own_blocks
    earlier = (peer[:, None] == peer[None, :]) & (order[None, :] < order[:, None])
    rank = jnp.sum(earlier.astype(jnp.int32), axis=1)
    spot = jnp.where(peer < row_count, peer * 2 + rank, -1)
    at = (spot[:, None] == order[None, :]).astype(jnp.int32)
    slot_at = jnp.sum(at * (order[:, None] + 1), axis=0) - 1
    local_at = jnp.sum(at * (tile_target[:, None] % own_blocks + 1), axis=0) - 1
    source_at = jnp.sum(at * (tile_source[:, None] + 1), axis=0) - 1
    holder = source_at // own_blocks
    dx = (holder // 4 - me // 4) % 4
    dy = (holder // 2 - me // 2) % 2
    dc = (holder - me) % 2
    inner = (dy * 4 + dx) * own_blocks + source_at % own_blocks
    places = 8 * own_blocks
    panel_at = jnp.where(source_at >= 0, dc * places + inner, -1)
    near_place = jnp.where((source_at >= 0) & (dc == 0), inner, places)
    cross_place = jnp.where((source_at >= 0) & (dc == 1), inner, places)

    def side_list(slot, place):
        used = (place < places).astype(jnp.int32)
        before = (order[None, :] < order[:, None]).astype(jnp.int32)
        used_before = jnp.sum(before * used[None, :], axis=1)
        count = jnp.sum(used).reshape(1)
        position = jnp.where(used > 0, used_before, count + order - used_before)
        chosen = (position[:, None] == order[None, :]).astype(jnp.int32)
        values = (jnp.maximum(slot, 0), order, place)
        return [count] + [jnp.sum(chosen * value[:, None], axis=0) for value in values]

    far = move(jnp.stack([slot_at, cross_place]), 0, 0, 1)
    lists = side_list(slot_at, near_place) + side_list(far[0], far[1])

    turned = jnp.swapaxes(adjacency, 1, 2)
    far_turned = move(turned, 0, 0, 1)
    marked = after(
        upstream * labels.astype(BF16)[:, None], turned, far_turned, *lists
    )

    def forward(shards, note):
        return pl.pallas_call(
            forward_kernel,
            out_shape=jax.ShapeDtypeStruct((row_count, 2 * block + note, share), BF16),
            in_specs=[SMEM_SPEC] * 3 + [ANY_SPEC] * (1 + len(shards)),
            out_specs=HBM_SPEC,
            scratch_shapes=[
                pltpu.VMEM((blk_count, own_rows, share), BF16),
                pltpu.VMEM(adjacency.shape, BF16),
                pltpu.VMEM((row_count, 2 * block + note, share), BF16),
                pltpu.SemaphoreType.DMA((blk_count + 1,)),
                pltpu.SemaphoreType.DMA((row_count,)),
            ],
            compiler_params=SMALL,
            cost_estimate=pl.CostEstimate(
                flops=2 * slots * block * block * share,
                bytes_accessed=2 * own_rows * blk_count * share,
                transcendentals=0,
            ),
        )(slot_at, panel_at, local_at, adjacency, *shards)

    def exchange(value):
        return lax.all_to_all(value, "rows", 0, 0, tiled=True)

    def spread(pair):
        return [move(pair, -1, 0, 0), move(pair, 1, 0, 0)]

    def both_cores(near, *others):
        held = near[:-1] + [after(near[-1], *others)]
        return near + [move(value, 0, 0, 1) for value in held]

    own = hidden[:, columns[0]]
    twice, across = move(own, 2, 0, 0), move(own, 0, 1, 0)
    pair = after(jnp.concatenate([own, across]), twice, slot_at, panel_at, local_at)
    pairs = spread(pair)
    near = [own, across, twice, move(twice, 0, 1, 0), *pairs]
    own = after(hidden[:, columns[1]], twice, across)
    across = move(own, 0, 1, 0)
    sums = forward(both_cores(near, across), NOTE)
    twice = move(after(own, *pairs), 2, 0, 0)
    got = [exchange(sums)]
    pairs = spread(after(jnp.concatenate([own, across]), sums, twice))
    near = [own, across, twice, move(twice, 0, 1, 0), *pairs]
    got.append(exchange(forward(both_cores(near), 0)))
    local_got = got[0][:, 2 * block : 2 * block + 2, 0].astype(jnp.int32).reshape(-1)

    early = [
        pl.pallas_call(
            lambda *refs: sum_kernel(block, *refs),
            out_shape=jax.ShapeDtypeStruct((own_rows, share), BF16),
            in_specs=[SMEM_SPEC, VMEM_SPEC],
            out_specs=VMEM_SPEC,
            scratch_shapes=[pltpu.VMEM((own_rows, share), F32)],
            compiler_params=SMALL,
            cost_estimate=pl.CostEstimate(
                flops=slots * block * share, bytes_accessed=2 * slots * block * share, transcendentals=0
            ),
        )(local_got, term)
        for term in got[:-1]
    ]
    last_sums, grad, send = pl.pallas_call(
        lambda *refs: owner_kernel(block, *refs),
        out_shape=(
            jax.ShapeDtypeStruct((own_rows, share), BF16),
            jax.ShapeDtypeStruct((own_rows, width), BF16),
            jax.ShapeDtypeStruct((row_count, 2 * block, share), BF16),
        ),
        in_specs=[SMEM_SPEC] + [VMEM_SPEC] * CHUNKS + [ANY_SPEC] * 2,
        out_specs=(HBM_SPEC,) * 3,
        scratch_shapes=[
            pltpu.VMEM((own_rows, share), F32),
            pltpu.VMEM((width, width), BF16),
            pltpu.VMEM((own_rows, width), BF16),
            pltpu.VMEM((own_rows, share), BF16),
            pltpu.VMEM((own_rows, width), BF16),
            pltpu.SemaphoreType.DMA((4,)),
            pltpu.SemaphoreType.DMA((slots,)),
        ],
        compiler_params=LARGE,
        cost_estimate=pl.CostEstimate(
            flops=2 * own_rows * width * width,
            bytes_accessed=10 * own_rows * width,
            transcendentals=own_rows * width,
        ),
    )(local_got, got[-1], *early, weight, marked)
    back = [exchange(send)]
    tail_rows = width // blk_count * CHUNKS
    output, *sends, local_grad = pl.pallas_call(
        lambda *refs: finish_kernel(block, *refs),
        out_shape=(
            jax.ShapeDtypeStruct((own_rows, width), BF16),
            *[
                jax.ShapeDtypeStruct((row_count, 2 * block + tail, share), BF16)
                for tail in [0] * (CHUNKS - 2) + [tail_rows]
            ],
            jax.ShapeDtypeStruct((width, width), F32),
        ),
        in_specs=[SMEM_SPEC] + [VMEM_SPEC] * (CHUNKS + 2),
        out_specs=(VMEM_SPEC,) * (CHUNKS + 1),
        compiler_params=LARGE,
        cost_estimate=pl.CostEstimate(
            flops=4 * own_rows * width * width,
            bytes_accessed=8 * own_rows * width,
            transcendentals=own_rows * width,
        ),
    )(local_got, *early, last_sums, grad, weight)

    def backward(near):
        far_near = move(near[:, : 2 * block, :], 0, 0, 1)
        return pl.pallas_call(
            lambda *refs: backward_kernel(block, *refs),
            out_shape=[
                jax.ShapeDtypeStruct((count * own_rows, share), BF16) for count in (1, 1, 1, 1, 2, 2)
            ],
            in_specs=[SMEM_SPEC] * 8 + [VMEM_SPEC] * 4,
            out_specs=[HBM_SPEC] * 6,
            scratch_shapes=[
                pltpu.VMEM(((places + 1) * block, share), F32),
                pltpu.VMEM((8, own_rows, share), BF16),
                pltpu.SemaphoreType.DMA((8,)),
            ],
            compiler_params=MIDDLE,
            cost_estimate=pl.CostEstimate(
                flops=2 * slots * block * block * share,
                bytes_accessed=2 * own_rows * blk_count * share,
                transcendentals=0,
            ),
        )(*lists, turned, far_turned, near, far_near)

    def wide_sum(*values):
        return sum(value.astype(F32) for value in values).astype(BF16)

    def first_sums(parts):
        own, across, twice, across_twice, plus, minus = parts
        from_minus, from_plus = move(plus, 1, 0, 0), move(minus, -1, 0, 0)
        twice = after(wide_sum(twice, move(across_twice, 0, 1, 0)), from_minus, from_plus)
        own = wide_sum(own, from_minus[:own_rows], from_plus[:own_rows])
        across = wide_sum(across, from_minus[own_rows:], from_plus[own_rows:])
        return [own, across, twice]

    def last_moves(parts):
        own, across, twice = parts
        return [own, move(across, 0, 1, 0), move(twice, 2, 0, 0)]

    x, y, c = me // 4, (me // 2) % 2, me % 2

    def halve(value, bit, dy, dc):
        half = value.shape[0] // 2
        keep = lax.dynamic_slice_in_dim(value, bit * half, half)
        return keep + move(lax.dynamic_slice_in_dim(value, (1 - bit) * half, half), 0, dy, dc)

    value = halve(halve(local_grad, c, 0, 1), y, 1, 0)
    rows = value.shape[0] // 4
    terms = [lax.dynamic_slice_in_dim(value, ((x + step) % 4) * rows, rows) for step in range(4)]
    piece = terms[0] + sum(move(terms[step], step, 0, 0) for step in (1, 2, 3))
    piece = jnp.concatenate([piece[:, cols] for cols in columns]).astype(BF16)
    sends[-1] = sends[-1].at[:, 2 * block :, :].set(piece[None])

    back.append(exchange(after(sends[-1], back[0])))
    piece = jnp.sum(back[-1][:, 2 * block :, :].astype(F32), axis=0)
    half_way = first_sums(backward(back[0]))
    last = backward(after(back[1], *half_way))
    received = last_moves(half_way)
    last_half_way = first_sums(after(tuple(last), *received))
    d_proj = [wide_sum(*received), wide_sum(*last_moves(last_half_way))]
    d_hidden = sum(
        lax.dot_general(
            part, weight[:, cols], (((1,), (1,)), ((), ())), preferred_element_type=F32
        )
        for part, cols in zip(d_proj, columns)
    ).astype(BF16)

    pieces = lax.all_to_all(
        jnp.broadcast_to(piece[None], (blk_count, *piece.shape)), "blk", 0, 0, tiled=True
    )
    pieces = pieces.reshape(4, 2, 2, CHUNKS, rows, share).transpose(2, 1, 0, 4, 3, 5)
    node_total = own_rows * row_count * blk_count
    d_weight = pieces.reshape(width, width) * (1.0 / math.sqrt(node_total))
    return (output, d_hidden, d_weight)


def solution(mesh):
    both = ("rows", "blk")
    return jax.shard_map(
        body,
        mesh=mesh,
        in_specs=(P(both, None), P(), P(both, None, None), P(both), P(both), P(both, None), P(both)),
        out_specs=(P(both, None), P(both, None), P()),
        check_vma=False,
    )
```

```python
import math

import jax
import jax.numpy as jnp
from jax import lax
from jax.experimental import pallas as pl
from jax.experimental.pallas import tpu as pltpu
from jax.sharding import PartitionSpec as P

BF16 = jnp.bfloat16
F32 = jnp.float32
CHUNKS = 2
NOTE = 16
GROUP = 4
SMEM_SPEC = pl.BlockSpec(memory_space=pltpu.SMEM)
VMEM_SPEC = pl.BlockSpec(memory_space=pltpu.VMEM)
ANY_SPEC = pl.BlockSpec(memory_space=pl.ANY)
HBM_SPEC = pl.BlockSpec(memory_space=pltpu.HBM)
MIB = 1024 * 1024
SMALL = pltpu.CompilerParams(vmem_limit_bytes=20 * MIB)
MIDDLE = pltpu.CompilerParams(vmem_limit_bytes=44 * MIB)
LARGE = pltpu.CompilerParams(vmem_limit_bytes=56 * MIB)


def after(value, *others):
    return lax.optimization_barrier((value, *others))[0]


def blk_pairs(blk_count, dx, dy, dc):
    x_count = blk_count // 4
    pairs = []
    for b in range(blk_count):
        x, y, c = b // 4, (b // 2) % 2, b % 2
        pairs.append((b, ((x + dx) % x_count) * 4 + ((y + dy) % 2) * 2 + (c + dc) % 2))
    return pairs


def run_all(copies):
    for copy in copies:
        copy.start()
    for copy in copies:
        copy.wait()


def forward_kernel(slot_ref, source_ref, local_ref, tiles_ref, *refs):
    shards, out_ref, (held, tiles, laid, sems, out_sems) = refs[:-6], refs[-6], refs[-5:]
    rows = held.shape[1]
    copies = [pltpu.make_async_copy(tiles_ref, tiles, sems.at[0])]
    side = len(shards) // 2
    for core in range(2):
        own, across, twice, across_twice, plus, minus = shards[core * side : (core + 1) * side]
        parts = [
            own, plus.at[pl.ds(0, rows)], twice, minus.at[pl.ds(0, rows)],
            across, plus.at[pl.ds(rows, rows)],
            across_twice, minus.at[pl.ds(rows, rows)],
        ]
        for part in parts:
            place = len(copies) - 1
            copies.append(pltpu.make_async_copy(part, held.at[place], sems.at[place + 1]))
    run_all(copies)
    block = tiles.shape[1]
    noted = out_ref.shape[1] > 2 * block
    row = lax.broadcasted_iota(jnp.int32, (NOTE, out_ref.shape[2]), 0)
    stores = []
    for p in range(out_ref.shape[0]):
        for j in range(2):
            slot = jnp.maximum(slot_ref[2 * p + j], 0)
            source = jnp.maximum(source_ref[2 * p + j], 0)
            panel = held[source // 8, pl.ds(pl.multiple_of((source % 8) * block, block), block), :]
            product = jnp.dot(tiles[slot], panel, preferred_element_type=F32)
            laid[p, j * block : (j + 1) * block, :] = product.astype(BF16)
        if noted:
            note = jnp.where(row == 0, local_ref[2 * p], local_ref[2 * p + 1])
            laid[p, 2 * block :, :] = note.astype(F32).astype(BF16)
        stores.append(pltpu.make_async_copy(laid.at[p], out_ref.at[p], out_sems.at[p]))
        stores[-1].start()
    for store in stores:
        store.wait()


def sum_terms(local_ref, term_ref, total, block):
    total[...] = jnp.zeros(total.shape, F32)

    def add(p, carry):
        for j in range(2):
            local = local_ref[2 * p + j]

            @pl.when(local >= 0)
            def _():
                rows = pl.ds(pl.multiple_of(local * block, block), block)
                total[rows, :] += term_ref[p, j * block : (j + 1) * block, :].astype(F32)

        return carry

    lax.fori_loop(0, term_ref.shape[0], add, 0)


def sum_kernel(block, local_ref, term_ref, out_ref, total):
    sum_terms(local_ref, term_ref, total, block)
    out_ref[...] = total[...].astype(BF16)


def owner_kernel(block, local_ref, term_ref, *refs):
    early, (weight_ref, up_ref, sum_ref, grad_ref, send_ref) = refs[: CHUNKS - 1], refs[CHUNKS - 1 : CHUNKS + 4]
    total, weight, up, last, grad, sems, send_sems = refs[CHUNKS + 4 :]
    loads = [
        pltpu.make_async_copy(weight_ref, weight, sems.at[0]),
        pltpu.make_async_copy(up_ref, up, sems.at[1]),
    ]
    for load in loads:
        load.start()
    total[...] = jnp.zeros(total.shape, F32)
    sum_terms(local_ref, term_ref, total, block)
    for load in loads:
        load.wait()
    early_stores = []
    for g in range(total.shape[0] // block):
        rows = slice(g * block, (g + 1) * block)
        last[rows, :] = total[rows, :].astype(BF16)
        summed = jnp.dot(
            jnp.concatenate([ref[rows, :] for ref in early] + [last[rows, :]], axis=1),
            weight[...],
            preferred_element_type=F32,
        )
        logistic = jax.nn.sigmoid(summed)
        slope = logistic * (1.0 + summed * (1.0 - logistic))
        grad[rows, :] = (up[rows, :].astype(F32) * slope).astype(BF16)
        part = pl.ds(g * block, block)
        for k, (value, ref) in enumerate(((last, sum_ref), (grad, grad_ref))):
            early_stores.append(
                pltpu.make_async_copy(value.at[part], ref.at[part], sems.at[2 + 2 * g + k])
            )
            early_stores[-1].start()
    width = send_ref.shape[2]
    stores = []
    for s in range(2 * send_ref.shape[0]):
        local = jnp.maximum(local_ref[s], 0)
        rows = pl.ds(pl.multiple_of(local * block, block), block)
        stores.append(
            pltpu.make_async_copy(
                grad.at[rows, pl.ds(0, width)],
                send_ref.at[s // 2, pl.ds(s % 2 * block, block)],
                send_sems.at[s],
            )
        )
    run_all(stores)
    for store in early_stores:
        store.wait()


def lay_out(local_ref, grad_ref, send_ref, chunk, block):
    width = send_ref.shape[2]
    cols = slice(chunk * width, (chunk + 1) * width)
    for p in range(send_ref.shape[0]):
        for j in range(2):
            local = jnp.maximum(local_ref[2 * p + j], 0)
            rows = pl.ds(pl.multiple_of(local * block, block), block)
            send_ref[p, j * block : (j + 1) * block, :] = grad_ref[rows, cols]


def finish_kernel(block, local_ref, *refs):
    parts, (grad_ref, weight_ref, out_ref), (*send_refs, dw_ref) = (
        refs[:CHUNKS],
        refs[CHUNKS : CHUNKS + 3],
        refs[CHUNKS + 3 :],
    )
    for k, send_ref in enumerate(send_refs):
        lay_out(local_ref, grad_ref, send_ref, k + 1, block)
    weight = weight_ref[...]
    dw = jnp.zeros(dw_ref.shape, F32)
    for g in range(out_ref.shape[0] // block):
        rows = slice(g * block, (g + 1) * block)
        aggregated = jnp.concatenate([ref[rows, :] for ref in parts], axis=1)
        summed = jnp.dot(aggregated, weight, preferred_element_type=F32)
        out_ref[rows, :] = (summed * jax.nn.sigmoid(summed)).astype(BF16)
        dw = dw + lax.dot_general(
            aggregated, grad_ref[rows, :], (((0,), (0,)), ((), ())), preferred_element_type=F32
        )
    dw_ref[...] = dw


def backward_kernel(block, *refs):
    lists, (near_tiles, far_tiles, near, far), outs = refs[:8], refs[8:12], refs[12:18]
    held, laid, sems = refs[18:]
    held[...] = jnp.zeros(held.shape, F32)
    for (count_ref, tile_ref, grad_ref, place_ref), tiles, grads in (
        (lists[:4], near_tiles, near),
        (lists[4:], far_tiles, far),
    ):

        def group(i, carry):
            entries = [i * GROUP + u for u in range(GROUP)]
            products = [
                jnp.dot(
                    tiles[tile_ref[e]],
                    grads[grad_ref[e] // 2, pl.ds(pl.multiple_of(grad_ref[e] % 2 * block, block), block), :],
                    preferred_element_type=F32,
                )
                for e in entries
            ]
            for e, product in zip(entries, products):
                held[pl.ds(pl.multiple_of(place_ref[e] * block, block), block), :] += product
            return carry

        lax.fori_loop(0, (count_ref[0] + GROUP - 1) // GROUP, group, 0)
    own, across, twice, across_twice, plus, minus = outs
    rows = own.shape[0]
    order = [
        own, plus.at[pl.ds(0, rows)], twice, minus.at[pl.ds(0, rows)],
        across, plus.at[pl.ds(rows, rows)], across_twice, minus.at[pl.ds(rows, rows)],
    ]
    stores = []
    for k, out in enumerate(order):
        laid[k] = held[k * rows : (k + 1) * rows, :].astype(BF16)
        stores.append(pltpu.make_async_copy(laid.at[k], out, sems.at[k]))
        stores[-1].start()
    for store in stores:
        store.wait()


def body(hidden, weight, adjacency, tile_target, tile_source, upstream, labels):
    block = adjacency.shape[1]
    slots = adjacency.shape[0]
    own_rows, width = hidden.shape
    own_blocks = own_rows // block
    row_count = lax.axis_size("rows")
    blk_count = lax.axis_size("blk")
    share = width // CHUNKS
    me = lax.axis_index("blk")
    columns = [slice(k * share, (k + 1) * share) for k in range(CHUNKS)]

    def move(value, dx, dy, dc):
        return lax.ppermute(value, "blk", blk_pairs(blk_count, dx, dy, dc))

    order = jnp.arange(slots, dtype=jnp.int32)
    peer = tile_target // own_blocks
    earlier = (peer[:, None] == peer[None, :]) & (order[None, :] < order[:, None])
    rank = jnp.sum(earlier.astype(jnp.int32), axis=1)
    spot = jnp.where(peer < row_count, peer * 2 + rank, -1)
    at = (spot[:, None] == order[None, :]).astype(jnp.int32)
    slot_at = jnp.sum(at * (order[:, None] + 1), axis=0) - 1
    local_at = jnp.sum(at * (tile_target[:, None] % own_blocks + 1), axis=0) - 1
    source_at = jnp.sum(at * (tile_source[:, None] + 1), axis=0) - 1
    holder = source_at // own_blocks
    dx = (holder // 4 - me // 4) % 4
    dy = (holder // 2 - me // 2) % 2
    dc = (holder - me) % 2
    inner = (dy * 4 + dx) * own_blocks + source_at % own_blocks
    places = 8 * own_blocks
    panel_at = jnp.where(source_at >= 0, dc * places + inner, -1)
    near_place = jnp.where((source_at >= 0) & (dc == 0), inner, places)
    cross_place = jnp.where((source_at >= 0) & (dc == 1), inner, places)

    def side_list(slot, place):
        used = (place < places).astype(jnp.int32)
        before = (order[None, :] < order[:, None]).astype(jnp.int32)
        used_before = jnp.sum(before * used[None, :], axis=1)
        count = jnp.sum(used).reshape(1)
        position = jnp.where(used > 0, used_before, count + order - used_before)
        chosen = (position[:, None] == order[None, :]).astype(jnp.int32)
        values = (jnp.maximum(slot, 0), order, place)
        return [count] + [jnp.sum(chosen * value[:, None], axis=0) for value in values]

    far = move(jnp.stack([slot_at, cross_place]), 0, 0, 1)
    lists = side_list(slot_at, near_place) + side_list(far[0], far[1])

    turned = jnp.swapaxes(adjacency, 1, 2)
    far_turned = move(turned, 0, 0, 1)
    marked = after(
        upstream * labels.astype(BF16)[:, None], turned, far_turned, *lists
    )

    def forward(shards, note):
        return pl.pallas_call(
            forward_kernel,
            out_shape=jax.ShapeDtypeStruct((row_count, 2 * block + note, share), BF16),
            in_specs=[SMEM_SPEC] * 3 + [ANY_SPEC] * (1 + len(shards)),
            out_specs=HBM_SPEC,
            scratch_shapes=[
                pltpu.VMEM((blk_count, own_rows, share), BF16),
                pltpu.VMEM(adjacency.shape, BF16),
                pltpu.VMEM((row_count, 2 * block + note, share), BF16),
                pltpu.SemaphoreType.DMA((blk_count + 1,)),
                pltpu.SemaphoreType.DMA((row_count,)),
            ],
            compiler_params=SMALL,
            cost_estimate=pl.CostEstimate(
                flops=2 * slots * block * block * share,
                bytes_accessed=2 * own_rows * blk_count * share,
                transcendentals=0,
            ),
        )(slot_at, panel_at, local_at, adjacency, *shards)

    def exchange(value):
        return lax.all_to_all(value, "rows", 0, 0, tiled=True)

    def spread(pair):
        return [move(pair, -1, 0, 0), move(pair, 1, 0, 0)]

    def both_cores(near, *others):
        held = near[:-1] + [after(near[-1], *others)]
        return near + [move(value, 0, 0, 1) for value in held]

    own = hidden[:, columns[0]]
    twice, across = move(own, 2, 0, 0), move(own, 0, 1, 0)
    pair = after(jnp.concatenate([own, across]), twice, slot_at, panel_at, local_at)
    pairs = spread(pair)
    near = [own, across, twice, move(twice, 0, 1, 0), *pairs]
    own = after(hidden[:, columns[1]], twice, across)
    across = move(own, 0, 1, 0)
    sums = forward(both_cores(near, across), NOTE)
    twice = move(after(own, *pairs), 2, 0, 0)
    got = [exchange(sums)]
    pairs = spread(after(jnp.concatenate([own, across]), sums, twice))
    near = [own, across, twice, move(twice, 0, 1, 0), *pairs]
    got.append(exchange(forward(both_cores(near), 0)))
    local_got = got[0][:, 2 * block : 2 * block + 2, 0].astype(jnp.int32).reshape(-1)

    early = [
        pl.pallas_call(
            lambda *refs: sum_kernel(block, *refs),
            out_shape=jax.ShapeDtypeStruct((own_rows, share), BF16),
            in_specs=[SMEM_SPEC, VMEM_SPEC],
            out_specs=VMEM_SPEC,
            scratch_shapes=[pltpu.VMEM((own_rows, share), F32)],
            compiler_params=SMALL,
            cost_estimate=pl.CostEstimate(
                flops=slots * block * share, bytes_accessed=2 * slots * block * share, transcendentals=0
            ),
        )(local_got, term)
        for term in got[:-1]
    ]
    last_sums, grad, send = pl.pallas_call(
        lambda *refs: owner_kernel(block, *refs),
        out_shape=(
            jax.ShapeDtypeStruct((own_rows, share), BF16),
            jax.ShapeDtypeStruct((own_rows, width), BF16),
            jax.ShapeDtypeStruct((row_count, 2 * block, share), BF16),
        ),
        in_specs=[SMEM_SPEC] + [VMEM_SPEC] * CHUNKS + [ANY_SPEC] * 2,
        out_specs=(HBM_SPEC,) * 3,
        scratch_shapes=[
            pltpu.VMEM((own_rows, share), F32),
            pltpu.VMEM((width, width), BF16),
            pltpu.VMEM((own_rows, width), BF16),
            pltpu.VMEM((own_rows, share), BF16),
            pltpu.VMEM((own_rows, width), BF16),
            pltpu.SemaphoreType.DMA((2 + 2 * own_blocks,)),
            pltpu.SemaphoreType.DMA((slots,)),
        ],
        compiler_params=LARGE,
        cost_estimate=pl.CostEstimate(
            flops=2 * own_rows * width * width,
            bytes_accessed=10 * own_rows * width,
            transcendentals=own_rows * width,
        ),
    )(local_got, got[-1], *early, weight, marked)
    back = [exchange(send)]
    tail_rows = width // blk_count * CHUNKS
    output, *sends, local_grad = pl.pallas_call(
        lambda *refs: finish_kernel(block, *refs),
        out_shape=(
            jax.ShapeDtypeStruct((own_rows, width), BF16),
            *[
                jax.ShapeDtypeStruct((row_count, 2 * block + tail, share), BF16)
                for tail in [0] * (CHUNKS - 2) + [tail_rows]
            ],
            jax.ShapeDtypeStruct((width, width), F32),
        ),
        in_specs=[SMEM_SPEC] + [VMEM_SPEC] * (CHUNKS + 2),
        out_specs=(VMEM_SPEC,) * (CHUNKS + 1),
        compiler_params=LARGE,
        cost_estimate=pl.CostEstimate(
            flops=4 * own_rows * width * width,
            bytes_accessed=8 * own_rows * width,
            transcendentals=own_rows * width,
        ),
    )(local_got, *early, last_sums, grad, weight)

    def backward(near):
        far_near = move(near[:, : 2 * block, :], 0, 0, 1)
        return pl.pallas_call(
            lambda *refs: backward_kernel(block, *refs),
            out_shape=[
                jax.ShapeDtypeStruct((count * own_rows, share), BF16) for count in (1, 1, 1, 1, 2, 2)
            ],
            in_specs=[SMEM_SPEC] * 8 + [VMEM_SPEC] * 4,
            out_specs=[HBM_SPEC] * 6,
            scratch_shapes=[
                pltpu.VMEM(((places + 1) * block, share), F32),
                pltpu.VMEM((8, own_rows, share), BF16),
                pltpu.SemaphoreType.DMA((8,)),
            ],
            compiler_params=MIDDLE,
            cost_estimate=pl.CostEstimate(
                flops=2 * slots * block * block * share,
                bytes_accessed=2 * own_rows * blk_count * share,
                transcendentals=0,
            ),
        )(*lists, turned, far_turned, near, far_near)

    def wide_sum(*values):
        return sum(value.astype(F32) for value in values).astype(BF16)

    def first_sums(parts):
        own, across, twice, across_twice, plus, minus = parts
        from_minus, from_plus = move(plus, 1, 0, 0), move(minus, -1, 0, 0)
        twice = after(wide_sum(twice, move(across_twice, 0, 1, 0)), from_minus, from_plus)
        own = wide_sum(own, from_minus[:own_rows], from_plus[:own_rows])
        across = wide_sum(across, from_minus[own_rows:], from_plus[own_rows:])
        return [own, across, twice]

    def last_moves(parts):
        own, across, twice = parts
        return [own, move(across, 0, 1, 0), move(twice, 2, 0, 0)]

    x, y, c = me // 4, (me // 2) % 2, me % 2

    def halve(value, bit, dy, dc):
        half = value.shape[0] // 2
        keep = lax.dynamic_slice_in_dim(value, bit * half, half)
        return keep + move(lax.dynamic_slice_in_dim(value, (1 - bit) * half, half), 0, dy, dc)

    value = halve(halve(local_grad, c, 0, 1), y, 1, 0)
    rows = value.shape[0] // 4
    terms = [lax.dynamic_slice_in_dim(value, ((x + step) % 4) * rows, rows) for step in range(4)]
    piece = terms[0] + sum(move(terms[step], step, 0, 0) for step in (1, 2, 3))
    piece = jnp.concatenate([piece[:, cols] for cols in columns]).astype(BF16)
    sends[-1] = sends[-1].at[:, 2 * block :, :].set(piece[None])

    back.append(exchange(after(sends[-1], back[0])))
    piece = jnp.sum(back[-1][:, 2 * block :, :].astype(F32), axis=0)
    half_way = first_sums(backward(back[0]))
    last = backward(after(back[1], *half_way))
    received = last_moves(half_way)
    last_half_way = first_sums(after(tuple(last), *received))
    d_proj = [wide_sum(*received), wide_sum(*last_moves(last_half_way))]
    d_hidden = sum(
        lax.dot_general(
            part, weight[:, cols], (((1,), (1,)), ((), ())), preferred_element_type=F32
        )
        for part, cols in zip(d_proj, columns)
    ).astype(BF16)

    pieces = lax.all_to_all(
        jnp.broadcast_to(piece[None], (blk_count, *piece.shape)), "blk", 0, 0, tiled=True
    )
    pieces = pieces.reshape(4, 2, 2, CHUNKS, rows, share).transpose(2, 1, 0, 4, 3, 5)
    node_total = own_rows * row_count * blk_count
    d_weight = pieces.reshape(width, width) * (1.0 / math.sqrt(node_total))
    return (output, d_hidden, d_weight)


def solution(mesh):
    both = ("rows", "blk")
    return jax.shard_map(
        body,
        mesh=mesh,
        in_specs=(P(both, None), P(), P(both, None, None), P(both), P(both), P(both, None), P(both)),
        out_specs=(P(both, None), P(both, None), P()),
        check_vma=False,
    )
```
